32 devices in a mesh: groups: 2 (over y), row: 4 (over z), col: 2 (over x), dp: 2 (over core).
Axes of the slice: x: 2, y: 2, z: 4, core: 2. Of those that a mesh axis runs over, the one named last changes fastest.
Arguments:
- tokens: bfloat16 [64, 6144], P(('groups', 'dp', 'row'), 'col'), parts along dimension 0, may hold values from -6 to 6
- cotangent: bfloat16 [64, 6144], P(('groups', 'dp', 'row'), 'col'), parts along dimension 0, may hold values from -6 to 6
- up_blocks: bfloat16 [4, 2, 576, 128, 128], P('row', 'col'), may hold values from -0.109375 to 0.109375
- down_blocks: bfloat16 [4, 2, 576, 128, 128], P('row', 'col'), may hold values from -0.0546875 to 0.0546875
- up_index: int32 [4, 2, 576, 2], P('row', 'col'), may hold values from 0 to 47, as said below
- down_index: int32 [4, 2, 576, 2], P('row', 'col'), may hold values from 0 to 47, as said below
- tile_counts: int32 [4, 2, 2], P('row', 'col'), may hold values from 432 to 576, as said below
- up_cover_rows: float32 [6144], P('col'), may hold values from 10 to 1000
- up_cover_cols: float32 [24576], P('row'), may hold values from 10 to 1000
- down_cover_rows: float32 [24576], P('row'), may hold values from 10 to 1000
- down_cover_cols: float32 [6144], P('col'), may hold values from 10 to 1000
Outputs:
- mixed: bfloat16 [64, 6144], P(('groups', 'dp', 'row'), 'col'), parts along dimension 0
- token_grad: bfloat16 [64, 6144], P(('groups', 'dp', 'row'), 'col'), parts along dimension 0
- up_step: bfloat16 [8, 2, 576, 128, 128], P(('groups', 'row'), 'col', 'dp'), parts along dimension 0
- down_step: bfloat16 [8, 2, 576, 128, 128], P(('groups', 'row'), 'col', 'dp'), parts along dimension 0
- up_rows_new: float32 [12288], P(('groups', 'col')), parts along dimension 0
- up_cols_new: float32 [49152], P(('groups', 'row')), parts along dimension 0
- down_rows_new: float32 [49152], P(('groups', 'row')), parts along dimension 0
- down_cols_new: float32 [12288], P(('groups', 'col')), parts along dimension 0
The draws below stay inside these ranges and needn't reach their ends.
There are 2 independent parts, one for each index of `groups`. The reference program is written for one: setup_inputs(seed, part) draws one part's arguments, and reference() takes and returns one part's arrays. A program takes and returns all parts, laid end to end along the dimension named above; an argument that names none is the same for every part. Nothing has to cross between parts.
Inputs may be any that keep to these rules, and one draw needn't show every extreme that they name: `up_index`: each tile's 576 slots name distinct blocks of its 24 x 48 blocks: entry 0 is the feature block (below 24), entry 1 the hidden-unit block (below 48). `down_index`: as for up_index, drawn independently. `tile_counts`: some tile is full in each weight.
All inputs are finite; a program needn't handle non-finite values.
Results may differ from the reference program's by a relative error of at most 0.015.
Values may be sent and summed in bfloat16 or wider, within the bound.
A program may use at most 384 MiB of HBM per device.

```python
import math
import jax
import jax.numpy as jnp
from jax import lax

BLK = 128
D = 6144
FF = 24576
GRID_ROWS = 4
GRID_COLS = 2
DBLK = 24
FBLK = 48
CAP = 576
TOKENS = 32
N_DP = 2


def draw_block_list(key):
    tile_total = GRID_ROWS * GRID_COLS
    tile_keys = jax.random.split(key, tile_total)
    places = DBLK * FBLK

    def tile_order(tile_key):
        return jax.random.permutation(tile_key, places)
    orders = jax.vmap(tile_order)(tile_keys)
    chosen = orders[:, :CAP].astype(jnp.int32)
    block_rows = chosen // FBLK
    block_cols = chosen % FBLK
    return jnp.stack([block_rows, block_cols], axis=-1).reshape(GRID_ROWS, GRID_COLS, CAP, 2).astype(jnp.int32)


def draw_up_index(key, part):
    key = jax.random.fold_in(key, 11)
    return draw_block_list(key)


def draw_down_index(key, part):
    key = jax.random.fold_in(key, 12)
    return draw_block_list(key)


def draw_tile_counts(key, part):
    key = jax.random.fold_in(key, 13)
    tile_total = GRID_ROWS * GRID_COLS
    low_count = CAP - CAP // 4
    key_counts, key_full, key_low = jax.random.split(key, 3)
    counts = jax.random.randint(key_counts, (tile_total, 2), low_count, CAP + 1).astype(jnp.int32)
    full_tile = jax.random.randint(key_full, (2,), 0, tile_total).astype(jnp.int32)
    low_shift = jax.random.randint(key_low, (2,), 1, max(tile_total, 2)).astype(jnp.int32)
    low_tile = (full_tile + low_shift) % tile_total
    columns = jnp.arange(2, dtype=jnp.int32)
    counts = counts.at[full_tile, columns].set(CAP)
    counts = counts.at[low_tile, columns].set(low_count)
    return counts.reshape(GRID_ROWS, GRID_COLS, 2).astype(jnp.int32)


def block_scale(own_key, extent, cuts, smallest, high):
    gain = 1.0
    for axis_at, parts in cuts:
        steps = jax.random.uniform(jax.random.fold_in(jax.random.fold_in(own_key, 6), axis_at), (parts,), jnp.float32, smallest / len(cuts), high / len(cuts))
        gain = gain * jnp.repeat(jnp.exp(steps), extent[axis_at] // parts).reshape((-1,) + (1,) * (len(extent) - 1 - axis_at))
    return gain


def centred(own_key, shape, scale, limit, pieces=(), kind=jnp.bfloat16):
    entries = jax.random.normal(own_key, shape, jnp.float32) * scale
    if len(pieces) > 0:
        entries = block_scale(own_key, shape, pieces, -0.22, 0.18) * entries
    return jnp.clip(entries, min=-limit, max=limit).astype(kind)


def setup_inputs(seed: int = 0, part: int = 0) -> dict:
    keys = jax.random.split(jax.random.key(seed), 12)
    own_keys = jax.random.split(jax.random.fold_in(keys[11], part), 12)
    tokens = centred(own_keys[0], (TOKENS, D), 1.0, 6.0, ((0, 8), (1, 2)))
    cotangent = centred(own_keys[1], (TOKENS, D), 1.0, 6.0, ((0, 8), (1, 2)))
    up_blocks = centred(keys[2], (GRID_ROWS, GRID_COLS, CAP, BLK, BLK), (D // 2) ** -0.5, 0.109375, ((0, 4), (1, 2)))
    down_blocks = centred(keys[3], (GRID_ROWS, GRID_COLS, CAP, BLK, BLK), (FF // 2) ** -0.5, 0.0546875, ((0, 4), (1, 2)))
    up_index = draw_up_index(jax.random.fold_in(keys[11], 71), part)
    down_index = draw_down_index(jax.random.fold_in(keys[11], 71), part)
    tile_counts = draw_tile_counts(jax.random.fold_in(keys[11], 71), part)
    up_cover_rows = jnp.clip(jnp.exp(math.log(1000.0) - 4.6051702 * jax.random.uniform(keys[7], (D,), jnp.float32) ** block_scale(keys[7], (D,), ((0, 2),), -0.2, 0.2)), 10.0, 1000.0)
    up_cover_cols = jnp.clip(jnp.exp(math.log(1000.0) - 4.6051702 * jax.random.uniform(keys[8], (FF,), jnp.float32) ** block_scale(keys[8], (FF,), ((0, 4),), -0.2, 0.2)), 10.0, 1000.0)
    down_cover_rows = jnp.clip(jnp.exp(math.log(1000.0) - 4.6051702 * jax.random.uniform(keys[9], (FF,), jnp.float32) ** block_scale(keys[9], (FF,), ((0, 4),), -0.2, 0.2)), 10.0, 1000.0)
    down_cover_cols = jnp.clip(jnp.exp(math.log(1000.0) - 4.6051702 * jax.random.uniform(keys[10], (D,), jnp.float32) ** block_scale(keys[10], (D,), ((0, 2),), -0.2, 0.2)), 10.0, 1000.0)
    return {"tokens": tokens, "cotangent": cotangent, "up_blocks": up_blocks, "down_blocks": down_blocks, "up_index": up_index, "down_index": down_index, "tile_counts": tile_counts, "up_cover_rows": up_cover_rows, "up_cover_cols": up_cover_cols, "down_cover_rows": down_cover_rows, "down_cover_cols": down_cover_cols}


precise = lax.Precision.HIGHEST

def rounded(values):
    return lax.optimization_barrier(values.astype(jnp.bfloat16)).astype(jnp.float32)

def silu_pair(hidden_pre):
    sigmoid_val = 1.0 / (1.0 + jnp.exp(-hidden_pre))
    return (hidden_pre * sigmoid_val, sigmoid_val * (1.0 + hidden_pre * (1.0 - sigmoid_val)))

def slot_map(positions, live_count, places):
    slot_ids = jnp.arange(positions.shape[0], dtype=jnp.int32)
    place_ids = jnp.arange(places, dtype=jnp.int32)
    matched = (positions[:, None] == place_ids[None, :]) & (slot_ids < live_count)[:, None]
    return matched.astype(jnp.float32)

def scatter_max(values, positions, places):
    matched = positions[:, None] == jnp.arange(places, dtype=jnp.int32)[None, :]
    return lax.optimization_barrier(jnp.max(jnp.where(matched[:, :, None], values[:, None, :], 0.0), axis=0)).reshape(-1)

def precondition(gradient, row_pos, col_pos, live_mask, row_cover, col_cover):
    width_block = gradient.shape[-1]
    row_side = jnp.take(row_cover.reshape(-1, width_block), row_pos, axis=0)
    col_side = jnp.take(col_cover.reshape(-1, width_block), col_pos, axis=0)
    second = jnp.minimum(row_side[:, :, None], col_side[:, None, :]) + gradient * gradient
    live_cube = live_mask[:, None, None]
    scaled = jnp.where(live_cube, gradient / jnp.sqrt(second), 0.0)
    largest = jnp.where(live_cube, second, 0.0)
    row_best = scatter_max(lax.optimization_barrier(jnp.max(largest, axis=2)), row_pos, row_cover.shape[0] // width_block)
    col_best = scatter_max(lax.optimization_barrier(jnp.max(largest, axis=1)), col_pos, col_cover.shape[0] // width_block)
    return (scaled.astype(jnp.bfloat16), jnp.maximum(row_cover, row_best), jnp.maximum(col_cover, col_best))

def tile_product(source, blocks, take_pos, put_pos, live_count, places, pattern):
    picked = jnp.take(source, take_pos, axis=2).astype(jnp.float32)
    product = jnp.einsum(pattern, picked, blocks.astype(jnp.float32), precision=precise)
    spread = slot_map(put_pos, live_count, places)
    return jnp.einsum('gtsk,sm->gtmk', product, spread, precision=precise)

def tile_gradient(left, right, left_pos, right_pos, live_count, pattern):
    left_picked = jnp.take(left, left_pos, axis=2).astype(jnp.float32)
    right_picked = jnp.take(right, right_pos, axis=2).astype(jnp.float32)
    per_group = jnp.einsum(pattern, left_picked, right_picked, precision=precise)
    summed = lax.optimization_barrier(jnp.sum(rounded(per_group), axis=0))
    slot_ids = jnp.arange(left_pos.shape[0], dtype=jnp.int32)
    return jnp.where((slot_ids < live_count)[:, None, None], summed, 0.0)

def reference(tokens, cotangent, up_blocks, down_blocks, up_index, down_index, tile_counts, up_cover_rows, up_cover_cols, down_cover_rows, down_cover_cols):
    group_tokens = TOKENS // N_DP
    row_ids = jnp.arange(GRID_ROWS, dtype=jnp.int32)

    def split_tokens(values):
        return values.reshape(N_DP, group_tokens, GRID_COLS, DBLK, BLK).transpose(2, 0, 1, 3, 4)

    def join_tokens(values):
        return values.transpose(1, 2, 0, 3, 4).reshape(TOKENS, D).astype(jnp.bfloat16)
    token_tiles = split_tokens(tokens)
    cot_tiles = split_tokens(cotangent)

    def hidden_row(row_id):

        def one_tile(source, blocks, positions, counts):
            return tile_product(source, blocks, positions[:, 0], positions[:, 1], counts[0], FBLK, 'gtsp,spq->gtsq')
        partials = jax.vmap(one_tile)(token_tiles, up_blocks[row_id], up_index[row_id], tile_counts[row_id])
        return lax.optimization_barrier(jnp.sum(rounded(partials), axis=0))
    hidden = lax.map(hidden_row, row_ids)
    act_float, slope = silu_pair(hidden)
    activation = act_float.astype(jnp.bfloat16)

    def mixed_step(running, row_id):

        def one_tile(blocks, positions, counts):
            return tile_product(activation[row_id], blocks, positions[:, 1], positions[:, 0], counts[1], DBLK, 'gtsq,sqp->gtsp')
        partials = jax.vmap(one_tile)(down_blocks[row_id], down_index[row_id], tile_counts[row_id])
        return (running + rounded(partials), None)
    empty_tiles = jnp.zeros((GRID_COLS, N_DP, group_tokens, DBLK, BLK), jnp.float32)
    mixed = join_tokens(lax.scan(mixed_step, empty_tiles, row_ids)[0])

    def dact_row(row_id):

        def one_tile(source, blocks, positions, counts):
            return tile_product(source, blocks, positions[:, 0], positions[:, 1], counts[1], FBLK, 'gtsp,sqp->gtsq')
        partials = jax.vmap(one_tile)(cot_tiles, down_blocks[row_id], down_index[row_id], tile_counts[row_id])
        return lax.optimization_barrier(jnp.sum(rounded(partials), axis=0))
    dact = lax.map(dact_row, row_ids)
    dhidden = (dact * slope).astype(jnp.bfloat16)

    def back_step(running, row_id):

        def one_tile(blocks, positions, counts):
            return tile_product(dhidden[row_id], blocks, positions[:, 1], positions[:, 0], counts[0], DBLK, 'gtsq,spq->gtsp')
        partials = jax.vmap(one_tile)(up_blocks[row_id], up_index[row_id], tile_counts[row_id])
        return (running + rounded(partials), None)
    token_grad = join_tokens(lax.scan(back_step, empty_tiles, row_ids)[0])
    feature_up_all = up_cover_rows.reshape(GRID_COLS, -1)
    feature_down_all = down_cover_cols.reshape(GRID_COLS, -1)
    unit_up_all = up_cover_cols.reshape(GRID_ROWS, -1)
    unit_down_all = down_cover_rows.reshape(GRID_ROWS, -1)

    def update_row(row_id):

        def update_tile(token_tile, cot_tile, up_pos, down_pos, counts, feature_up, feature_down):
            slot_ids = jnp.arange(CAP, dtype=jnp.int32)
            up_grad = tile_gradient(token_tile, dhidden[row_id], up_pos[:, 0], up_pos[:, 1], counts[0], 'gtsp,gtsq->gspq')
            down_grad = tile_gradient(activation[row_id], cot_tile, down_pos[:, 1], down_pos[:, 0], counts[1], 'gtsq,gtsp->gsqp')
            up_out = precondition(up_grad, up_pos[:, 0], up_pos[:, 1], slot_ids < counts[0], feature_up, unit_up_all[row_id])
            down_out = precondition(down_grad, down_pos[:, 1], down_pos[:, 0], slot_ids < counts[1], unit_down_all[row_id], feature_down)
            return up_out + down_out
        return jax.vmap(update_tile)(token_tiles, cot_tiles, up_index[row_id], down_index[row_id], tile_counts[row_id], feature_up_all, feature_down_all)
    up_step, up_feature, up_unit, down_step, down_unit, down_feature = lax.map(update_row, row_ids)
    up_rows_new = lax.optimization_barrier(jnp.max(up_feature, axis=0)).reshape(D)
    up_cols_new = lax.optimization_barrier(jnp.max(up_unit, axis=1)).reshape(FF)
    down_rows_new = lax.optimization_barrier(jnp.max(down_unit, axis=1)).reshape(FF)
    down_cols_new = lax.optimization_barrier(jnp.max(down_feature, axis=0)).reshape(D)
    return (mixed, token_grad, up_step, down_step, up_rows_new, up_cols_new, down_rows_new, down_cols_new)
```

```python
import functools

import jax
import jax.numpy as jnp
from jax import lax
from jax.experimental import pallas as pl
from jax.experimental.pallas import tpu as pltpu
from jax.sharding import PartitionSpec as P

MESH = pl.DeviceIdType.MESH
VMEM_LIMIT = 56 * 1024 * 1024
NN = (((1,), (0,)), ((), ()))
NT = (((1,), (1,)), ((), ()))


def largest_divisor(total, most):
    return max(d for d in range(1, most + 1) if total % d == 0)


def dot(left, right, dims):
    return lax.dot_general(left, right, dims, preferred_element_type=jnp.float32)


def slot_places(index_ref, slot, live, features, units):
    alive = slot < live
    feature = jnp.where(alive, index_ref[2 * slot], features)
    unit = jnp.where(alive, index_ref[2 * slot + 1], units)
    return feature, unit


def first_kernel(
    chunk, batch, up_at, down_at, counts, place, x_ref, up_ref, down_ref, out_ref, hid, dac
):
    step = pl.program_id(0)
    features = x_ref.shape[1] - 1
    units = hid.shape[0] - 1
    shares, _, _, share_rows, _ = out_ref.shape

    @pl.when(step == 0)
    def _():
        hid[...] = jnp.zeros_like(hid)
        dac[...] = jnp.zeros_like(dac)

    first = place[0] * (chunk * pl.num_programs(0)) + step * chunk

    @pl.loop(0, chunk // batch)
    def _(part):
        work = []
        for j in range(batch):
            at = part * batch + j
            slot = first + at
            uf, uu = slot_places(up_at, slot, counts[0], features, units)
            df, du = slot_places(down_at, slot, counts[1], features, units)
            work.append((uu, dot(x_ref[0, uf], up_ref[at], NN), hid))
            work.append((du, dot(x_ref[1, df], down_ref[at], NT), dac))
        for unit, product, total in work:
            total[unit] += product

    @pl.when(step == pl.num_programs(0) - 1)
    def _():
        for share in range(shares):
            rows = pl.ds(share * share_rows, share_rows)
            out_ref[share, 0] = hid[:units, rows, :].astype(jnp.bfloat16)
            out_ref[share, 1] = dac[:units, rows, :].astype(jnp.bfloat16)


def first_products(up_at, down_at, counts, place, x, up_weight, down_weight, units, shares):
    slots = up_weight.shape[0] // shares
    _, features1, tokens, width = x.shape
    chunk = largest_divisor(slots, 24)
    batch = largest_divisor(chunk, 8)
    steps = slots // chunk
    weight = pl.BlockSpec(
        (chunk, width, width), lambda i, a, b, c, p: (p[0] * steps + i, 0, 0)
    )
    return pl.pallas_call(
        functools.partial(first_kernel, chunk, batch),
        grid_spec=pltpu.PrefetchScalarGridSpec(
            num_scalar_prefetch=4,
            grid=(steps,),
            in_specs=[
                pl.BlockSpec(x.shape, lambda i, a, b, c, p: (0, 0, 0, 0)),
                weight,
                weight,
            ],
            out_specs=pl.BlockSpec(
                (shares, 2, units, tokens // shares, width), lambda i, a, b, c, p: (0, 0, 0, 0, 0)
            ),
            scratch_shapes=[
                pltpu.VMEM((units + 1, tokens, width), jnp.float32),
                pltpu.VMEM((units + 1, tokens, width), jnp.float32),
            ],
        ),
        out_shape=jax.ShapeDtypeStruct(
            (shares, 2, units, tokens // shares, width), jnp.bfloat16
        ),
        compiler_params=pltpu.CompilerParams(vmem_limit_bytes=VMEM_LIMIT),
        cost_estimate=pl.CostEstimate(
            flops=4 * slots * tokens * width * width,
            bytes_accessed=4 * slots * width * width,
            transcendentals=0,
        ),
    )(up_at, down_at, counts, place, x, up_weight, down_weight)


def second_kernel(
    chunk,
    batch,
    up_at,
    down_at,
    counts,
    place,
    x_ref,
    h_ref,
    up_ref,
    down_ref,
    f_cover,
    u_cover,
    up_step,
    down_step,
    sums_ref,
    f_new,
    u_new,
    x_turned,
    act_turned,
    dh,
    act,
    f_rows,
    u_rows,
    f_rows_max,
    u_rows_max,
    f_cols,
    u_cols,
    f_cols_max,
    u_cols_max,
    mix,
    tok,
):
    step = pl.program_id(0)
    features = x_ref.shape[1] - 1
    units = h_ref.shape[1]
    width = x_ref.shape[-1]
    groups = width // 8

    @pl.when(step == 0)
    def _():
        mix[...] = jnp.zeros_like(mix)
        tok[...] = jnp.zeros_like(tok)
        dh[units] = jnp.zeros_like(dh[units])
        act[units] = jnp.zeros_like(act[units])
        act_turned[units] = jnp.zeros_like(act_turned[units])
        x_turned[features] = jnp.zeros_like(x_turned[features])
        f_rows[features] = jnp.ones_like(f_rows[features])
        u_rows[units] = jnp.ones_like(u_rows[units])
        f_cols[features] = jnp.ones_like(f_cols[features])
        u_cols[units] = jnp.ones_like(u_cols[units])
        f_cols_max[...] = jnp.zeros_like(f_cols_max)
        u_cols_max[...] = jnp.zeros_like(u_cols_max)

        @pl.loop(0, features)
        def _(f):
            x_turned[f] = x_ref[0, f].astype(jnp.float32).T.astype(jnp.bfloat16)
            wide = jnp.broadcast_to(f_cover[0, pl.ds(f, 1)], (width, width)).T
            f_rows[f] = wide
            f_rows_max[f] = wide
            f_cols[f] = f_cover[1, pl.ds(f, 1)]

        @pl.loop(0, units)
        def _(u):
            act[u] = h_ref[0, u]
            dh[u] = h_ref[1, u]
            act_turned[u] = h_ref[0, u].astype(jnp.float32).T.astype(jnp.bfloat16)
            wide = jnp.broadcast_to(u_cover[1, pl.ds(u, 1)], (width, width)).T
            u_rows[u] = wide
            u_rows_max[u] = wide
            u_cols[u] = u_cover[0, pl.ds(u, 1)]

    first = place[0] * (chunk * pl.num_programs(0)) + step * chunk

    def one_step(grad, rows, cols, rows_max, cols_max, row, col, step_ref, at):
        second = jnp.minimum(rows[row], cols[col]) + grad * grad
        step_ref[0, 0, at] = (grad * lax.rsqrt(second)).astype(jnp.bfloat16)
        rows_max[row] = jnp.maximum(rows_max[row], second)
        best = jnp.max(second.reshape(groups, 8, width), axis=0)
        cols_max[col] = jnp.maximum(cols_max[col], best)

    @pl.loop(0, chunk // batch)
    def _(part):
        work = []
        for j in range(batch):
            at = part * batch + j
            slot = first + at
            uf, uu = slot_places(up_at, slot, counts[0], features, units)
            df, du = slot_places(down_at, slot, counts[1], features, units)
            work.append((uf, dot(dh[uu], up_ref[at], NT), tok))
            work.append((df, dot(act[du], down_ref[at], NN), mix))
        for feature, product, total in work:
            total[feature] += product
        for j in range(batch):
            at = part * batch + j
            slot = first + at
            uf, uu = slot_places(up_at, slot, counts[0], features, units)
            df, du = slot_places(down_at, slot, counts[1], features, units)
            up_grad = dot(x_turned[uf], dh[uu], NN)
            down_grad = dot(act_turned[du], x_ref[1, df], NN)
            one_step(up_grad, f_rows, u_cols, f_rows_max, u_cols_max, uf, uu, up_step, at)
            one_step(down_grad, u_rows, f_cols, u_rows_max, f_cols_max, du, df, down_step, at)

    @pl.when(step == pl.num_programs(0) - 1)
    def _():
        sums_ref[0] = mix[:features].astype(jnp.bfloat16)
        sums_ref[1] = tok[:features].astype(jnp.bfloat16)

        @pl.loop(0, features)
        def _(f):
            f_new[0, pl.ds(f, 1)] = jnp.max(f_rows_max[f].T, axis=0, keepdims=True)
            best = jnp.max(f_cols_max[f], axis=0, keepdims=True)
            f_new[1, pl.ds(f, 1)] = jnp.maximum(best, f_cols[f])

        @pl.loop(0, units)
        def _(u):
            u_new[1, pl.ds(u, 1)] = jnp.max(u_rows_max[u].T, axis=0, keepdims=True)
            best = jnp.max(u_cols_max[u], axis=0, keepdims=True)
            u_new[0, pl.ds(u, 1)] = jnp.maximum(best, u_cols[u])


def second_products(
    up_at, down_at, counts, place, x, h, up_weight, down_weight, f_cover, u_cover, shares
):
    slots = up_weight.shape[0] // shares
    _, features1, tokens, width = x.shape
    features = features1 - 1
    units = h.shape[1]
    chunk = largest_divisor(slots, 24)
    batch = largest_divisor(chunk, 4)
    steps = slots // chunk
    weight = pl.BlockSpec(
        (chunk, width, width), lambda i, a, b, c, p: (p[0] * steps + i, 0, 0)
    )
    stepped = pl.BlockSpec(
        (1, 1, chunk, width, width), lambda i, a, b, c, p: (0, 0, i, 0, 0)
    )

    def whole(shape):
        return pl.BlockSpec(shape, lambda i, a, b, c, p: (0,) * len(shape))

    f32, bf16 = jnp.float32, jnp.bfloat16
    sums = (2, features, tokens, width)
    return pl.pallas_call(
        functools.partial(second_kernel, chunk, batch),
        grid_spec=pltpu.PrefetchScalarGridSpec(
            num_scalar_prefetch=4,
            grid=(steps,),
            in_specs=[
                whole(x.shape),
                whole(h.shape),
                weight,
                weight,
                whole(f_cover.shape),
                whole(u_cover.shape),
            ],
            out_specs=[stepped, stepped, whole(sums), whole(f_cover.shape), whole(u_cover.shape)],
            scratch_shapes=[
                pltpu.VMEM((features + 1, width, tokens), bf16),
                pltpu.VMEM((units + 1, width, tokens), bf16),
                pltpu.VMEM((units + 1, tokens, width), bf16),
                pltpu.VMEM((units + 1, tokens, width), bf16),
                pltpu.VMEM((features + 1, width, width), f32),
                pltpu.VMEM((units + 1, width, width), f32),
                pltpu.VMEM((features + 1, width, width), f32),
                pltpu.VMEM((units + 1, width, width), f32),
                pltpu.VMEM((features + 1, 1, width), f32),
                pltpu.VMEM((units + 1, 1, width), f32),
                pltpu.VMEM((features + 1, 8, width), f32),
                pltpu.VMEM((units + 1, 8, width), f32),
                pltpu.VMEM((features + 1, tokens, width), f32),
                pltpu.VMEM((features + 1, tokens, width), f32),
            ],
        ),
        out_shape=[
            jax.ShapeDtypeStruct((1, 1, slots, width, width), bf16),
            jax.ShapeDtypeStruct((1, 1, slots, width, width), bf16),
            jax.ShapeDtypeStruct(sums, bf16),
            jax.ShapeDtypeStruct(f_cover.shape, f32),
            jax.ShapeDtypeStruct(u_cover.shape, f32),
        ],
        compiler_params=pltpu.CompilerParams(vmem_limit_bytes=VMEM_LIMIT),
        cost_estimate=pl.CostEstimate(
            flops=8 * slots * tokens * width * width,
            bytes_accessed=8 * slots * width * width,
            transcendentals=2 * slots * width * width,
        ),
    )(up_at, down_at, counts, place, x, h, up_weight, down_weight, f_cover, u_cover)


def gather_inputs(own):
    return lax.all_gather(own, ("dp", "row"), axis=0, tiled=False)


def silu_pair(hidden):
    sigma = 1.0 / (1.0 + jnp.exp(-hidden))
    return hidden * sigma, sigma * (1.0 + hidden * (1.0 - sigma))


def hidden_exchange(partial):
    mine = lax.psum_scatter(partial, "dp", scatter_dimension=0, tiled=False)
    total = lax.psum(mine, "col").astype(jnp.float32)
    activation, slope = silu_pair(total[0])
    both = jnp.stack([activation, total[1] * slope]).astype(jnp.bfloat16)
    return lax.all_gather(both, "dp", axis=2, tiled=True)


def final_exchange(sums, f_new, u_new):
    own = lax.psum_scatter(sums, ("dp", "row"), scatter_dimension=0, tiled=False)
    return own, lax.pmax(f_new, ("row", "dp")), lax.pmax(u_new, ("col", "dp"))


def on_device(
    tokens,
    cotangent,
    up_blocks,
    down_blocks,
    up_index,
    down_index,
    tile_counts,
    up_cover_rows,
    up_cover_cols,
    down_cover_rows,
    down_cover_cols,
):
    width = up_blocks.shape[-1]
    own_tokens = tokens.shape[0]
    features = tokens.shape[1] // width
    units = up_cover_cols.shape[0] // width
    shares = lax.axis_size("dp")
    rows = lax.axis_size("row")
    all_tokens = own_tokens * rows * shares

    up_at = up_index.reshape(-1)
    down_at = down_index.reshape(-1)
    counts = tile_counts.reshape(-1)
    place = lax.axis_index("dp").astype(jnp.int32).reshape(1)
    up_weight = up_blocks.reshape(up_blocks.shape[2:])
    down_weight = down_blocks.reshape(down_blocks.shape[2:])

    own = jnp.stack([tokens, cotangent]).reshape(2 * own_tokens * features, width)
    gathered = gather_inputs(own).reshape(shares * rows, 2, own_tokens, features, width)
    x = gathered.transpose(1, 3, 0, 2, 4).reshape(2, features, all_tokens, width)
    x = jnp.pad(x, ((0, 0), (0, 1), (0, 0), (0, 0)))

    partial = first_products(
        up_at, down_at, counts, place, x, up_weight, down_weight, units, shares
    )
    h = hidden_exchange(partial)

    f_cover = jnp.stack([up_cover_rows, down_cover_cols]).reshape(2, features, width)
    u_cover = jnp.stack([up_cover_cols, down_cover_rows]).reshape(2, units, width)
    up_step, down_step, sums, f_new, u_new = second_products(
        up_at, down_at, counts, place, x, h, up_weight, down_weight, f_cover, u_cover, shares
    )
    sums = sums.reshape(2, features, shares * rows, own_tokens, width).transpose(2, 0, 3, 1, 4)
    sums = sums.reshape(shares * rows, 2 * own_tokens * features, width)
    out, f_new, u_new = final_exchange(sums, f_new, u_new)
    out = out.reshape(2, own_tokens, features * width)
    f_new = f_new.reshape(2, features * width)
    u_new = u_new.reshape(2, units * width)
    return (out[0], out[1], up_step, down_step, f_new[0], u_new[0], u_new[1], f_new[1])


def solution(mesh):
    in_specs = (
        P(("groups", "dp", "row"), "col"),
        P(("groups", "dp", "row"), "col"),
        P("row", "col", None, None, None),
        P("row", "col", None, None, None),
        P("row", "col", None, None),
        P("row", "col", None, None),
        P("row", "col", None),
        P("col"),
        P("row"),
        P("row"),
        P("col"),
    )
    out_specs = (
        P(("groups", "dp", "row"), "col"),
        P(("groups", "dp", "row"), "col"),
        P(("groups", "row"), "col", "dp", None, None),
        P(("groups", "row"), "col", "dp", None, None),
        P(("groups", "col")),
        P(("groups", "row")),
        P(("groups", "row")),
        P(("groups", "col")),
    )
    return jax.shard_map(
        on_device, mesh=mesh, in_specs=in_specs, out_specs=out_specs, check_vma=False
    )
```

```python
import functools

import jax
import jax.numpy as jnp
from jax import lax
from jax.experimental import pallas as pl
from jax.experimental.pallas import tpu as pltpu
from jax.sharding import PartitionSpec as P

MESH = pl.DeviceIdType.MESH
VMEM_LIMIT = 56 * 1024 * 1024
NN = (((1,), (0,)), ((), ()))
NT = (((1,), (1,)), ((), ()))


def largest_divisor(total, most):
    return max(d for d in range(1, most + 1) if total % d == 0)


def dot(left, right, dims):
    return lax.dot_general(left, right, dims, preferred_element_type=jnp.float32)


def slot_places(index_ref, slot, live, features, units):
    alive = slot < live
    feature = jnp.where(alive, index_ref[2 * slot], features)
    unit = jnp.where(alive, index_ref[2 * slot + 1], units)
    return feature, unit


def first_kernel(
    chunk, batch, up_at, down_at, counts, place, x_ref, up_ref, down_ref, out_ref, hid, dac
):
    step = pl.program_id(0)
    features = x_ref.shape[1] - 1
    units = hid.shape[0] - 1
    shares, _, _, share_rows, _ = out_ref.shape

    @pl.when(step == 0)
    def _():
        hid[...] = jnp.zeros_like(hid)
        dac[...] = jnp.zeros_like(dac)

    first = place[0] * (chunk * pl.num_programs(0)) + step * chunk

    @pl.loop(0, chunk // batch)
    def _(part):
        work = []
        for j in range(batch):
            at = part * batch + j
            slot = first + at
            uf, uu = slot_places(up_at, slot, counts[0], features, units)
            df, du = slot_places(down_at, slot, counts[1], features, units)
            work.append((uu, dot(x_ref[0, uf], up_ref[at], NN), hid))
            work.append((du, dot(x_ref[1, df], down_ref[at], NT), dac))
        for unit, product, total in work:
            total[unit] += product

    @pl.when(step == pl.num_programs(0) - 1)
    def _():
        for share in range(shares):
            rows = pl.ds(share * share_rows, share_rows)
            out_ref[share, 0] = hid[:units, rows, :].astype(jnp.bfloat16)
            out_ref[share, 1] = dac[:units, rows, :].astype(jnp.bfloat16)


def first_products(up_at, down_at, counts, place, x, up_weight, down_weight, units, shares):
    slots = up_weight.shape[0] // shares
    _, features1, tokens, width = x.shape
    chunk = largest_divisor(slots, 24)
    batch = largest_divisor(chunk, 8)
    steps = slots // chunk
    weight = pl.BlockSpec(
        (chunk, width, width), lambda i, a, b, c, p: (p[0] * steps + i, 0, 0)
    )
    return pl.pallas_call(
        functools.partial(first_kernel, chunk, batch),
        grid_spec=pltpu.PrefetchScalarGridSpec(
            num_scalar_prefetch=4,
            grid=(steps,),
            in_specs=[
                pl.BlockSpec(x.shape, lambda i, a, b, c, p: (0, 0, 0, 0)),
                weight,
                weight,
            ],
            out_specs=pl.BlockSpec(
                (shares, 2, units, tokens // shares, width), lambda i, a, b, c, p: (0, 0, 0, 0, 0)
            ),
            scratch_shapes=[
                pltpu.VMEM((units + 1, tokens, width), jnp.float32),
                pltpu.VMEM((units + 1, tokens, width), jnp.float32),
            ],
        ),
        out_shape=jax.ShapeDtypeStruct(
            (shares, 2, units, tokens // shares, width), jnp.bfloat16
        ),
        compiler_params=pltpu.CompilerParams(vmem_limit_bytes=VMEM_LIMIT),
        cost_estimate=pl.CostEstimate(
            flops=4 * slots * tokens * width * width,
            bytes_accessed=4 * slots * width * width,
            transcendentals=0,
        ),
    )(up_at, down_at, counts, place, x, up_weight, down_weight)


def second_kernel(
    chunk,
    batch,
    up_at,
    down_at,
    counts,
    place,
    x_ref,
    h_ref,
    up_ref,
    down_ref,
    f_cover,
    u_cover,
    up_step,
    down_step,
    sums_ref,
    f_new,
    u_new,
    x_turned,
    act_turned,
    dh,
    act,
    f_rows,
    u_rows,
    f_rows_max,
    u_rows_max,
    f_cols,
    u_cols,
    f_cols_max,
    u_cols_max,
    mix,
    tok,
):
    step = pl.program_id(0)
    features = x_ref.shape[1] - 1
    shares, _, units, share_rows, _ = h_ref.shape
    width = x_ref.shape[-1]
    groups = width // 8

    @pl.when(step == 0)
    def _():
        mix[...] = jnp.zeros_like(mix)
        tok[...] = jnp.zeros_like(tok)
        dh[units] = jnp.zeros_like(dh[units])
        act[units] = jnp.zeros_like(act[units])
        act_turned[units] = jnp.zeros_like(act_turned[units])
        x_turned[features] = jnp.zeros_like(x_turned[features])
        f_rows[features] = jnp.ones_like(f_rows[features])
        u_rows[units] = jnp.ones_like(u_rows[units])
        f_cols[features] = jnp.ones_like(f_cols[features])
        u_cols[units] = jnp.ones_like(u_cols[units])
        f_cols_max[...] = jnp.zeros_like(f_cols_max)
        u_cols_max[...] = jnp.zeros_like(u_cols_max)

        @pl.loop(0, features)
        def _(f):
            x_turned[f] = x_ref[0, f].astype(jnp.float32).T.astype(jnp.bfloat16)
            wide = jnp.broadcast_to(f_cover[0, pl.ds(f, 1)], (width, width)).T
            f_rows[f] = wide
            f_rows_max[f] = wide
            f_cols[f] = f_cover[1, pl.ds(f, 1)]

        @pl.loop(0, units)
        def _(u):
            for share in range(shares):
                at = pl.ds(share * share_rows, share_rows)
                act[u, at] = h_ref[share, 0, u]
                dh[u, at] = h_ref[share, 1, u]
            act_turned[u] = act[u].astype(jnp.float32).T.astype(jnp.bfloat16)
            wide = jnp.broadcast_to(u_cover[1, pl.ds(u, 1)], (width, width)).T
            u_rows[u] = wide
            u_rows_max[u] = wide
            u_cols[u] = u_cover[0, pl.ds(u, 1)]

    first = place[0] * (chunk * pl.num_programs(0)) + step * chunk

    def one_step(grad, rows, cols, rows_max, cols_max, row, col, step_ref, at):
        second = jnp.minimum(rows[row], cols[col]) + grad * grad
        step_ref[0, 0, at] = (grad * lax.rsqrt(second)).astype(jnp.bfloat16)
        rows_max[row] = jnp.maximum(rows_max[row], second)
        best = jnp.max(second.reshape(groups, 8, width), axis=0)
        cols_max[col] = jnp.maximum(cols_max[col], best)

    @pl.loop(0, chunk // batch)
    def _(part):
        work = []
        for j in range(batch):
            at = part * batch + j
            slot = first + at
            uf, uu = slot_places(up_at, slot, counts[0], features, units)
            df, du = slot_places(down_at, slot, counts[1], features, units)
            work.append((uf, dot(dh[uu], up_ref[at], NT), tok))
            work.append((df, dot(act[du], down_ref[at], NN), mix))
        for feature, product, total in work:
            total[feature] += product
        for j in range(batch):
            at = part * batch + j
            slot = first + at
            uf, uu = slot_places(up_at, slot, counts[0], features, units)
            df, du = slot_places(down_at, slot, counts[1], features, units)
            up_grad = dot(x_turned[uf], dh[uu], NN)
            down_grad = dot(act_turned[du], x_ref[1, df], NN)
            one_step(up_grad, f_rows, u_cols, f_rows_max, u_cols_max, uf, uu, up_step, at)
            one_step(down_grad, u_rows, f_cols, u_rows_max, f_cols_max, du, df, down_step, at)

    @pl.when(step == pl.num_programs(0) - 1)
    def _():
        sums_ref[0] = mix[:features].astype(jnp.bfloat16)
        sums_ref[1] = tok[:features].astype(jnp.bfloat16)

        @pl.loop(0, features)
        def _(f):
            f_new[0, pl.ds(f, 1)] = jnp.max(f_rows_max[f].T, axis=0, keepdims=True)
            best = jnp.max(f_cols_max[f], axis=0, keepdims=True)
            f_new[1, pl.ds(f, 1)] = jnp.maximum(best, f_cols[f])

        @pl.loop(0, units)
        def _(u):
            u_new[1, pl.ds(u, 1)] = jnp.max(u_rows_max[u].T, axis=0, keepdims=True)
            best = jnp.max(u_cols_max[u], axis=0, keepdims=True)
            u_new[0, pl.ds(u, 1)] = jnp.maximum(best, u_cols[u])


def second_products(
    up_at, down_at, counts, place, x, h, up_weight, down_weight, f_cover, u_cover, shares
):
    slots = up_weight.shape[0] // shares
    _, features1, tokens, width = x.shape
    features = features1 - 1
    units = h.shape[2]
    chunk = largest_divisor(slots, 24)
    batch = largest_divisor(chunk, 4)
    steps = slots // chunk
    weight = pl.BlockSpec(
        (chunk, width, width), lambda i, a, b, c, p: (p[0] * steps + i, 0, 0)
    )
    stepped = pl.BlockSpec(
        (1, 1, chunk, width, width), lambda i, a, b, c, p: (0, 0, i, 0, 0)
    )

    def whole(shape):
        return pl.BlockSpec(shape, lambda i, a, b, c, p: (0,) * len(shape))

    f32, bf16 = jnp.float32, jnp.bfloat16
    sums = (2, features, tokens, width)
    return pl.pallas_call(
        functools.partial(second_kernel, chunk, batch),
        grid_spec=pltpu.PrefetchScalarGridSpec(
            num_scalar_prefetch=4,
            grid=(steps,),
            in_specs=[
                whole(x.shape),
                whole(h.shape),
                weight,
                weight,
                whole(f_cover.shape),
                whole(u_cover.shape),
            ],
            out_specs=[stepped, stepped, whole(sums), whole(f_cover.shape), whole(u_cover.shape)],
            scratch_shapes=[
                pltpu.VMEM((features + 1, width, tokens), bf16),
                pltpu.VMEM((units + 1, width, tokens), bf16),
                pltpu.VMEM((units + 1, tokens, width), bf16),
                pltpu.VMEM((units + 1, tokens, width), bf16),
                pltpu.VMEM((features + 1, width, width), f32),
                pltpu.VMEM((units + 1, width, width), f32),
                pltpu.VMEM((features + 1, width, width), f32),
                pltpu.VMEM((units + 1, width, width), f32),
                pltpu.VMEM((features + 1, 1, width), f32),
                pltpu.VMEM((units + 1, 1, width), f32),
                pltpu.VMEM((features + 1, 8, width), f32),
                pltpu.VMEM((units + 1, 8, width), f32),
                pltpu.VMEM((features + 1, tokens, width), f32),
                pltpu.VMEM((features + 1, tokens, width), f32),
            ],
        ),
        out_shape=[
            jax.ShapeDtypeStruct((1, 1, slots, width, width), bf16),
            jax.ShapeDtypeStruct((1, 1, slots, width, width), bf16),
            jax.ShapeDtypeStruct(sums, bf16),
            jax.ShapeDtypeStruct(f_cover.shape, f32),
            jax.ShapeDtypeStruct(u_cover.shape, f32),
        ],
        compiler_params=pltpu.CompilerParams(vmem_limit_bytes=VMEM_LIMIT),
        cost_estimate=pl.CostEstimate(
            flops=8 * slots * tokens * width * width,
            bytes_accessed=8 * slots * width * width,
            transcendentals=2 * slots * width * width,
        ),
    )(up_at, down_at, counts, place, x, h, up_weight, down_weight, f_cover, u_cover)


def silu_pair(hidden):
    sigma = 1.0 / (1.0 + jnp.exp(-hidden))
    return hidden * sigma, sigma * (1.0 + hidden * (1.0 - sigma))


def others(axis):
    size, me = lax.axis_size(axis), lax.axis_index(axis)
    return [{axis: lax.rem(me + k, size)} for k in range(1, size)]


def meet(devices):
    barrier = pltpu.get_barrier_semaphore()
    for device in devices:
        pl.semaphore_signal(barrier, inc=1, device_id=device, device_id_type=MESH)
    pl.semaphore_wait(barrier, len(devices))


def send(source, target, send_sem, recv_sem, device):
    copy = pltpu.make_async_remote_copy(
        src_ref=source,
        dst_ref=target,
        send_sem=send_sem,
        recv_sem=recv_sem,
        device_id=device,
        device_id_type=MESH,
    )
    copy.start()
    return copy


def comm_call(kernel, name, collective_id, out_shape, scratch_shapes, args):
    outs = jax.tree.map(lambda _: pl.BlockSpec(memory_space=pltpu.VMEM), out_shape)
    return pl.pallas_call(
        kernel,
        name=name,
        out_shape=out_shape,
        in_specs=[pl.BlockSpec(memory_space=pltpu.VMEM)] * len(args),
        out_specs=outs,
        scratch_shapes=scratch_shapes,
        compiler_params=pltpu.CompilerParams(
            collective_id=collective_id, has_side_effects=True, vmem_limit_bytes=VMEM_LIMIT
        ),
    )(*args)


def gather_kernel(own_ref, out_ref, row_send, row_recv, dp_send, dp_recv):
    size, me, share = lax.axis_size("row"), lax.axis_index("row"), lax.axis_index("dp")
    peers, partner = others("row"), others("dp")[0]
    meet(peers + [partner])
    mine = out_ref.at[share * size + me]
    row_copies = [
        send(own_ref, mine, row_send.at[k], row_recv.at[k], peer) for k, peer in enumerate(peers)
    ]
    dp_copies = [send(own_ref, mine, dp_send.at[size - 1], dp_recv.at[size - 1], partner)]
    out_ref[share * size + me] = own_ref[...]
    for k, copy in enumerate(row_copies):
        copy.wait_recv()
        landed = out_ref.at[share * size + lax.rem(me + size - k - 1, size)]
        dp_copies.append(send(landed, landed, dp_send.at[k], dp_recv.at[k], partner))
    for copy in dp_copies:
        copy.wait_recv()
    for copy in row_copies + dp_copies:
        copy.wait_send()


def gather_inputs(own):
    size = lax.axis_size("row")
    dma = pltpu.SemaphoreType.DMA
    return comm_call(
        gather_kernel,
        "gather_inputs",
        0,
        jax.ShapeDtypeStruct((2 * size,) + own.shape, own.dtype),
        [dma((size,)), dma((size,)), dma((size,)), dma((size,))],
        (own,),
    )


def hidden_kernel(
    pieces,
    part_ref,
    h_ref,
    from_dp,
    mine,
    from_col,
    dp_send,
    dp_recv,
    col_send,
    col_recv,
    last_send,
    last_recv,
):
    share = lax.axis_index("dp")
    peers, partner = others("col"), others("dp")[0]
    depth = part_ref.shape[2] // pieces
    meet(peers + [partner])
    cuts = [pl.ds(c * depth, depth) for c in range(pieces)]
    dp_copies = [
        send(
            part_ref.at[1 - share, :, cut],
            from_dp.at[:, cut],
            dp_send.at[c],
            dp_recv.at[c],
            partner,
        )
        for c, cut in enumerate(cuts)
    ]
    col_copies = []
    for c, cut in enumerate(cuts):
        dp_copies[c].wait_recv()
        total = part_ref[share, :, cut].astype(jnp.float32) + from_dp[:, cut].astype(jnp.float32)
        mine[:, cut] = total.astype(jnp.bfloat16)
        col_copies.append(
            [
                send(
                    mine.at[:, cut],
                    from_col.at[k, :, cut],
                    col_send.at[c, k],
                    col_recv.at[c, k],
                    peer,
                )
                for k, peer in enumerate(peers)
            ]
        )
    last_copies = []
    for c, cut in enumerate(cuts):
        total = mine[:, cut].astype(jnp.float32)
        for k, copy in enumerate(col_copies[c]):
            copy.wait_recv()
            total = total + from_col[k, :, cut].astype(jnp.float32)
        activation, slope = silu_pair(total[0])
        h_ref[share, 0, cut] = activation.astype(jnp.bfloat16)
        h_ref[share, 1, cut] = (total[1] * slope).astype(jnp.bfloat16)
        done = h_ref.at[share, :, cut]
        last_copies.append(send(done, done, last_send.at[c], last_recv.at[c], partner))
    for copy in last_copies:
        copy.wait_recv()
    for copy in dp_copies + sum(col_copies, []) + last_copies:
        copy.wait_send()


def hidden_exchange(partial):
    pieces = largest_divisor(partial.shape[2], 6)
    peers = lax.axis_size("col") - 1
    dma = pltpu.SemaphoreType.DMA
    piece = partial.shape[1:]
    return comm_call(
        functools.partial(hidden_kernel, pieces),
        "hidden_exchange",
        1,
        jax.ShapeDtypeStruct(partial.shape, jnp.bfloat16),
        [
            pltpu.VMEM(piece, jnp.bfloat16),
            pltpu.VMEM(piece, jnp.bfloat16),
            pltpu.VMEM((peers,) + piece, jnp.bfloat16),
            dma((pieces,)),
            dma((pieces,)),
            dma((pieces, peers)),
            dma((pieces, peers)),
            dma((pieces,)),
            dma((pieces,)),
        ],
        (partial,),
    )


def final_kernel(
    sums_ref,
    f_ref,
    u_ref,
    out_ref,
    f_out,
    u_out,
    from_dp,
    to_row,
    from_row,
    f_dp,
    u_dp,
    f_row,
    u_col,
    dp_send,
    dp_recv,
    row_send,
    row_recv,
    max_send,
    max_recv,
    f_send,
    f_recv,
    u_send,
    u_recv,
):
    size, me, share = lax.axis_size("row"), lax.axis_index("row"), lax.axis_index("dp")
    peers, columns, partner = others("row"), others("col"), others("dp")[0]
    meet(peers + columns + [partner])
    targets = [lax.rem(me + k, size) for k in range(1, size)] + [me]
    dp_copies = [
        send(
            sums_ref.at[(1 - share) * size + target],
            from_dp.at[k],
            dp_send.at[k],
            dp_recv.at[k],
            partner,
        )
        for k, target in enumerate(targets)
    ]
    max_copies = [
        send(f_ref, f_dp, max_send.at[0], max_recv.at[0], partner),
        send(u_ref, u_dp, max_send.at[1], max_recv.at[1], partner),
    ]
    row_copies = []
    for k, target in enumerate(targets):
        dp_copies[k].wait_recv()
        total = sums_ref[share * size + target].astype(jnp.float32)
        total = total + from_dp[k].astype(jnp.float32)
        if k < size - 1:
            to_row[k] = total.astype(jnp.bfloat16)
            row_copies.append(
                send(to_row.at[k], from_row.at[k], row_send.at[k], row_recv.at[k], peers[k])
            )
    max_copies[0].wait_recv()
    max_copies[0].wait_send()
    f_out[...] = jnp.maximum(f_ref[...], f_dp[...])
    max_copies[1].wait_recv()
    max_copies[1].wait_send()
    u_out[...] = jnp.maximum(u_ref[...], u_dp[...])
    f_own = f_out[...]
    f_dp[...] = f_own
    u_own = u_out[...]
    u_dp[...] = u_own
    f_copies = [
        send(f_dp, f_row.at[k], f_send.at[k], f_recv.at[k], peer) for k, peer in enumerate(peers)
    ]
    u_copies = [
        send(u_dp, u_col.at[k], u_send.at[k], u_recv.at[k], peer) for k, peer in enumerate(columns)
    ]
    for k, copy in enumerate(u_copies):
        copy.wait_recv()
        u_own = jnp.maximum(u_own, u_col[k])
    u_out[...] = u_own
    for k, copy in enumerate(row_copies):
        copy.wait_recv()
        total = total + from_row[k].astype(jnp.float32)
    out_ref[...] = total.astype(jnp.bfloat16)
    for k, copy in enumerate(f_copies):
        copy.wait_recv()
        f_own = jnp.maximum(f_own, f_row[k])
    f_out[...] = f_own
    for copy in dp_copies + row_copies + f_copies + u_copies:
        copy.wait_send()


def final_exchange(sums, f_new, u_new):
    size, columns = lax.axis_size("row"), lax.axis_size("col")
    dma = pltpu.SemaphoreType.DMA
    f32, bf16 = jnp.float32, jnp.bfloat16
    piece = sums.shape[1:]
    return comm_call(
        final_kernel,
        "final_exchange",
        2,
        (
            jax.ShapeDtypeStruct(piece, bf16),
            jax.ShapeDtypeStruct(f_new.shape, f32),
            jax.ShapeDtypeStruct(u_new.shape, f32),
        ),
        [
            pltpu.VMEM((size,) + piece, bf16),
            pltpu.VMEM((size - 1,) + piece, bf16),
            pltpu.VMEM((size - 1,) + piece, bf16),
            pltpu.VMEM(f_new.shape, f32),
            pltpu.VMEM(u_new.shape, f32),
            pltpu.VMEM((size - 1,) + f_new.shape, f32),
            pltpu.VMEM((columns - 1,) + u_new.shape, f32),
            dma((size,)),
            dma((size,)),
            dma((size - 1,)),
            dma((size - 1,)),
            dma((2,)),
            dma((2,)),
            dma((size - 1,)),
            dma((size - 1,)),
            dma((columns - 1,)),
            dma((columns - 1,)),
        ],
        (sums, f_new, u_new),
    )


def on_device(
    tokens,
    cotangent,
    up_blocks,
    down_blocks,
    up_index,
    down_index,
    tile_counts,
    up_cover_rows,
    up_cover_cols,
    down_cover_rows,
    down_cover_cols,
):
    width = up_blocks.shape[-1]
    own_tokens = tokens.shape[0]
    features = tokens.shape[1] // width
    units = up_cover_cols.shape[0] // width
    shares = lax.axis_size("dp")
    rows = lax.axis_size("row")
    all_tokens = own_tokens * rows * shares

    up_at = up_index.reshape(-1)
    down_at = down_index.reshape(-1)
    counts = tile_counts.reshape(-1)
    place = lax.axis_index("dp").astype(jnp.int32).reshape(1)
    up_weight = up_blocks.reshape(up_blocks.shape[2:])
    down_weight = down_blocks.reshape(down_blocks.shape[2:])

    own = jnp.stack([tokens, cotangent]).reshape(2 * own_tokens * features, width)
    gathered = gather_inputs(own).reshape(shares * rows, 2, own_tokens, features, width)
    x = gathered.transpose(1, 3, 0, 2, 4).reshape(2, features, all_tokens, width)
    x = jnp.pad(x, ((0, 0), (0, 1), (0, 0), (0, 0)))

    partial = first_products(
        up_at, down_at, counts, place, x, up_weight, down_weight, units, shares
    )
    h = hidden_exchange(partial)

    f_cover = jnp.stack([up_cover_rows, down_cover_cols]).reshape(2, features, width)
    u_cover = jnp.stack([up_cover_cols, down_cover_rows]).reshape(2, units, width)
    up_step, down_step, sums, f_new, u_new = second_products(
        up_at, down_at, counts, place, x, h, up_weight, down_weight, f_cover, u_cover, shares
    )
    sums = sums.reshape(2, features, shares * rows, own_tokens, width).transpose(2, 0, 3, 1, 4)
    sums = sums.reshape(shares * rows, 2 * own_tokens * features, width)
    out, f_new, u_new = final_exchange(sums, f_new, u_new)
    out = out.reshape(2, own_tokens, features * width)
    f_new = f_new.reshape(2, features * width)
    u_new = u_new.reshape(2, units * width)
    return (out[0], out[1], up_step, down_step, f_new[0], u_new[0], u_new[1], f_new[1])


def solution(mesh):
    in_specs = (
        P(("groups", "dp", "row"), "col"),
        P(("groups", "dp", "row"), "col"),
        P("row", "col", None, None, None),
        P("row", "col", None, None, None),
        P("row", "col", None, None),
        P("row", "col", None, None),
        P("row", "col", None),
        P("col"),
        P("row"),
        P("row"),
        P("col"),
    )
    out_specs = (
        P(("groups", "dp", "row"), "col"),
        P(("groups", "dp", "row"), "col"),
        P(("groups", "row"), "col", "dp", None, None),
        P(("groups", "row"), "col", "dp", None, None),
        P(("groups", "col")),
        P(("groups", "row")),
        P(("groups", "row")),
        P(("groups", "col")),
    )
    return jax.shard_map(
        on_device, mesh=mesh, in_specs=in_specs, out_specs=out_specs, check_vma=False
    )
```

```python
import functools

import jax
import jax.numpy as jnp
from jax import lax
from jax.experimental import pallas as pl
from jax.experimental.pallas import tpu as pltpu
from jax.sharding import PartitionSpec as P

MESH = pl.DeviceIdType.MESH
VMEM_LIMIT = 56 * 1024 * 1024
NN = (((1,), (0,)), ((), ()))
NT = (((1,), (1,)), ((), ()))


def largest_divisor(total, most):
    return max(d for d in range(1, most + 1) if total % d == 0)


def dot(left, right, dims):
    return lax.dot_general(left, right, dims, preferred_element_type=jnp.float32)


def slot_places(index_ref, slot, live, features, units):
    alive = slot < live
    read = index_ref[2 * slot]
    feature = jnp.where(alive, read, features)
    unit = jnp.where(alive, index_ref[2 * slot + 1], units)
    return read, feature, unit


def first_kernel(
    chunk, batch, up_at, down_at, counts, place, x_ref, up_ref, down_ref, out_ref, hid, dac
):
    step = pl.program_id(0)
    features = x_ref.shape[1]
    units = hid.shape[0] - 1
    shares, _, _, share_rows, _ = out_ref.shape

    @pl.when(step == 0)
    def _():
        hid[...] = jnp.zeros_like(hid)
        dac[...] = jnp.zeros_like(dac)

    first = place[0] * (chunk * pl.num_programs(0)) + step * chunk

    @pl.loop(0, chunk // batch)
    def _(part):
        work = []
        for j in range(batch):
            at = part * batch + j
            slot = first + at
            ux, uf, uu = slot_places(up_at, slot, counts[0], features, units)
            dx, df, du = slot_places(down_at, slot, counts[1], features, units)
            work.append((uu, dot(x_ref[0, ux], up_ref[at], NN), hid))
            work.append((du, dot(x_ref[1, dx], down_ref[at], NT), dac))
        for unit, product, total in work:
            total[unit] += product

    @pl.when(step == pl.num_programs(0) - 1)
    def _():
        for share in range(shares):
            rows = pl.ds(share * share_rows, share_rows)
            out_ref[share, 0] = hid[:units, rows, :].astype(jnp.bfloat16)
            out_ref[share, 1] = dac[:units, rows, :].astype(jnp.bfloat16)


def first_products(up_at, down_at, counts, place, x, up_weight, down_weight, units, shares):
    slots = up_weight.shape[0] // shares
    _, _, tokens, width = x.shape
    chunk = largest_divisor(slots, 48)
    batch = chunk
    steps = slots // chunk
    weight = pl.BlockSpec(
        (chunk, width, width), lambda i, a, b, c, p: (p[0] * steps + i, 0, 0)
    )
    return pl.pallas_call(
        functools.partial(first_kernel, chunk, batch),
        grid_spec=pltpu.PrefetchScalarGridSpec(
            num_scalar_prefetch=4,
            grid=(steps,),
            in_specs=[
                pl.BlockSpec(x.shape, lambda i, a, b, c, p: (0, 0, 0, 0)),
                weight,
                weight,
            ],
            out_specs=pl.BlockSpec(
                (shares, 2, units, tokens // shares, width), lambda i, a, b, c, p: (0, 0, 0, 0, 0)
            ),
            scratch_shapes=[
                pltpu.VMEM((units + 1, tokens, width), jnp.float32),
                pltpu.VMEM((units + 1, tokens, width), jnp.float32),
            ],
        ),
        out_shape=jax.ShapeDtypeStruct(
            (shares, 2, units, tokens // shares, width), jnp.bfloat16
        ),
        compiler_params=pltpu.CompilerParams(vmem_limit_bytes=VMEM_LIMIT),
        cost_estimate=pl.CostEstimate(
            flops=4 * slots * tokens * width * width,
            bytes_accessed=4 * slots * width * width,
            transcendentals=0,
        ),
    )(up_at, down_at, counts, place, x, up_weight, down_weight)


def second_kernel(
    chunk,
    batch,
    up_at,
    down_at,
    counts,
    place,
    x_ref,
    h_ref,
    up_ref,
    down_ref,
    up_rows,
    up_cols,
    down_rows,
    down_cols,
    up_step,
    down_step,
    sums_ref,
    up_rows_new,
    up_cols_new,
    down_rows_new,
    down_cols_new,
    x_turned,
    act_turned,
    dh,
    act,
    f_rows,
    u_rows,
    f_rows_max,
    u_rows_max,
    f_cols,
    u_cols,
    f_cols_max,
    u_cols_max,
    mix,
    tok,
):
    step = pl.program_id(0)
    features = x_ref.shape[1]
    shares, _, units, share_rows, _ = h_ref.shape
    width = x_ref.shape[-1]
    groups = width // 8

    @pl.when(step == 0)
    def _():
        mix[...] = jnp.zeros_like(mix)
        tok[...] = jnp.zeros_like(tok)
        dh[units] = jnp.zeros_like(dh[units])
        act[units] = jnp.zeros_like(act[units])
        act_turned[units] = jnp.zeros_like(act_turned[units])
        x_turned[features] = jnp.zeros_like(x_turned[features])
        f_rows[features] = jnp.ones_like(f_rows[features])
        u_rows[units] = jnp.ones_like(u_rows[units])
        f_cols[features] = jnp.ones_like(f_cols[features])
        u_cols[units] = jnp.ones_like(u_cols[units])
        f_cols_max[...] = jnp.zeros_like(f_cols_max)
        u_cols_max[...] = jnp.zeros_like(u_cols_max)

        @pl.loop(0, features, unroll=largest_divisor(features, 8))
        def _(f):
            x_turned[f] = x_ref[0, f].astype(jnp.float32).T.astype(jnp.bfloat16)
            wide = jnp.broadcast_to(up_rows[pl.ds(f, 1)], (width, width)).T
            f_rows[f] = wide
            f_rows_max[f] = wide
            f_cols[f] = down_cols[pl.ds(f, 1)]

        @pl.loop(0, units, unroll=largest_divisor(units, 8))
        def _(u):
            for share in range(shares):
                at = pl.ds(share * share_rows, share_rows)
                act[u, at] = h_ref[share, 0, u]
                dh[u, at] = h_ref[share, 1, u]
            act_turned[u] = act[u].astype(jnp.float32).T.astype(jnp.bfloat16)
            wide = jnp.broadcast_to(down_rows[pl.ds(u, 1)], (width, width)).T
            u_rows[u] = wide
            u_rows_max[u] = wide
            u_cols[u] = up_cols[pl.ds(u, 1)]

    first = place[0] * (chunk * pl.num_programs(0)) + step * chunk

    def one_step(grad, rows, cols, rows_max, cols_max, row, col, step_ref, at):
        second = jnp.minimum(rows[row], cols[col]) + grad * grad
        step_ref[0, 0, at] = (grad * lax.rsqrt(second)).astype(jnp.bfloat16)
        rows_max[row] = jnp.maximum(rows_max[row], second)
        best = jnp.max(second.reshape(groups, 8, width), axis=0)
        cols_max[col] = jnp.maximum(cols_max[col], best)

    @pl.loop(0, chunk // batch)
    def _(part):
        work = []
        for j in range(batch):
            at = part * batch + j
            slot = first + at
            ux, uf, uu = slot_places(up_at, slot, counts[0], features, units)
            dx, df, du = slot_places(down_at, slot, counts[1], features, units)
            work.append((uf, dot(dh[uu], up_ref[at], NT), tok))
            work.append((df, dot(act[du], down_ref[at], NN), mix))
        for feature, product, total in work:
            total[feature] += product
        for j in range(batch):
            at = part * batch + j
            slot = first + at
            ux, uf, uu = slot_places(up_at, slot, counts[0], features, units)
            dx, df, du = slot_places(down_at, slot, counts[1], features, units)
            up_grad = dot(x_turned[uf], dh[uu], NN)
            down_grad = dot(act_turned[du], x_ref[1, dx], NN)
            one_step(up_grad, f_rows, u_cols, f_rows_max, u_cols_max, uf, uu, up_step, at)
            one_step(down_grad, u_rows, f_cols, u_rows_max, f_cols_max, du, df, down_step, at)

    @pl.when(step == pl.num_programs(0) - 1)
    def _():
        sums_ref[0] = mix[:features].astype(jnp.bfloat16)
        sums_ref[1] = tok[:features].astype(jnp.bfloat16)

        @pl.loop(0, features, unroll=largest_divisor(features, 8))
        def _(f):
            up_rows_new[pl.ds(f, 1)] = jnp.max(f_rows_max[f].T, axis=0, keepdims=True)
            best = jnp.max(f_cols_max[f], axis=0, keepdims=True)
            down_cols_new[pl.ds(f, 1)] = jnp.maximum(best, f_cols[f])

        @pl.loop(0, units, unroll=largest_divisor(units, 8))
        def _(u):
            down_rows_new[pl.ds(u, 1)] = jnp.max(u_rows_max[u].T, axis=0, keepdims=True)
            best = jnp.max(u_cols_max[u], axis=0, keepdims=True)
            up_cols_new[pl.ds(u, 1)] = jnp.maximum(best, u_cols[u])


def second_products(
    up_at, down_at, counts, place, x, h, up_weight, down_weight, covers, shares
):
    slots = up_weight.shape[0] // shares
    _, features, tokens, width = x.shape
    units = h.shape[2]
    chunk = largest_divisor(slots, 24)
    batch = chunk
    steps = slots // chunk
    weight = pl.BlockSpec(
        (chunk, width, width), lambda i, a, b, c, p: (p[0] * steps + i, 0, 0)
    )
    stepped = pl.BlockSpec(
        (1, 1, chunk, width, width), lambda i, a, b, c, p: (0, 0, i, 0, 0)
    )

    def whole(shape):
        return pl.BlockSpec(shape, lambda i, a, b, c, p: (0,) * len(shape))

    f32, bf16 = jnp.float32, jnp.bfloat16
    sums = (2, features, tokens, width)
    return pl.pallas_call(
        functools.partial(second_kernel, chunk, batch),
        grid_spec=pltpu.PrefetchScalarGridSpec(
            num_scalar_prefetch=4,
            grid=(steps,),
            in_specs=[
                whole(x.shape),
                whole(h.shape),
                weight,
                weight,
                *[whole(cover.shape) for cover in covers],
            ],
            out_specs=[
                stepped,
                stepped,
                whole(sums),
                *[whole(cover.shape) for cover in covers],
            ],
            scratch_shapes=[
                pltpu.VMEM((features + 1, width, tokens), bf16),
                pltpu.VMEM((units + 1, width, tokens), bf16),
                pltpu.VMEM((units + 1, tokens, width), bf16),
                pltpu.VMEM((units + 1, tokens, width), bf16),
                pltpu.VMEM((features + 1, width, width), f32),
                pltpu.VMEM((units + 1, width, width), f32),
                pltpu.VMEM((features + 1, width, width), f32),
                pltpu.VMEM((units + 1, width, width), f32),
                pltpu.VMEM((features + 1, 1, width), f32),
                pltpu.VMEM((units + 1, 1, width), f32),
                pltpu.VMEM((features + 1, 8, width), f32),
                pltpu.VMEM((units + 1, 8, width), f32),
                pltpu.VMEM((features + 1, tokens, width), f32),
                pltpu.VMEM((features + 1, tokens, width), f32),
            ],
        ),
        out_shape=[
            jax.ShapeDtypeStruct((1, 1, slots, width, width), bf16),
            jax.ShapeDtypeStruct((1, 1, slots, width, width), bf16),
            jax.ShapeDtypeStruct(sums, bf16),
            *[jax.ShapeDtypeStruct(cover.shape, f32) for cover in covers],
        ],
        compiler_params=pltpu.CompilerParams(vmem_limit_bytes=VMEM_LIMIT),
        cost_estimate=pl.CostEstimate(
            flops=8 * slots * tokens * width * width,
            bytes_accessed=8 * slots * width * width,
            transcendentals=2 * slots * width * width,
        ),
    )(up_at, down_at, counts, place, x, h, up_weight, down_weight, *covers)


def silu_pair(hidden):
    sigma = 1.0 / (1.0 + jnp.exp(-hidden))
    return hidden * sigma, sigma * (1.0 + hidden * (1.0 - sigma))


def others(axis):
    size, me = lax.axis_size(axis), lax.axis_index(axis)
    return [{axis: lax.rem(me + k, size)} for k in range(1, size)]


def meet(devices):
    barrier = pltpu.get_barrier_semaphore()
    for device in devices:
        pl.semaphore_signal(barrier, inc=1, device_id=device, device_id_type=MESH)
    pl.semaphore_wait(barrier, len(devices))


def send(source, target, send_sem, recv_sem, device):
    copy = pltpu.make_async_remote_copy(
        src_ref=source,
        dst_ref=target,
        send_sem=send_sem,
        recv_sem=recv_sem,
        device_id=device,
        device_id_type=MESH,
    )
    copy.start()
    return copy


def comm_call(kernel, name, collective_id, out_shape, scratch_shapes, args):
    outs = jax.tree.map(lambda _: pl.BlockSpec(memory_space=pltpu.VMEM), out_shape)
    return pl.pallas_call(
        kernel,
        name=name,
        out_shape=out_shape,
        in_specs=[pl.BlockSpec(memory_space=pltpu.VMEM)] * len(args),
        out_specs=outs,
        scratch_shapes=scratch_shapes,
        compiler_params=pltpu.CompilerParams(
            collective_id=collective_id, has_side_effects=True, vmem_limit_bytes=VMEM_LIMIT
        ),
    )(*args)


def gather_kernel(own_ref, out_ref, row_send, row_recv, dp_send, dp_recv):
    size, me, share = lax.axis_size("row"), lax.axis_index("row"), lax.axis_index("dp")
    peers, partner = others("row"), others("dp")[0]
    meet(peers + [partner])
    mine = out_ref.at[share * size + me]
    row_copies = [
        send(own_ref, mine, row_send.at[k], row_recv.at[k], peer) for k, peer in enumerate(peers)
    ]
    dp_copies = [send(own_ref, mine, dp_send.at[size - 1], dp_recv.at[size - 1], partner)]
    out_ref[share * size + me] = own_ref[...]
    for k, copy in enumerate(row_copies):
        copy.wait_recv()
        landed = out_ref.at[share * size + lax.rem(me + size - k - 1, size)]
        dp_copies.append(send(landed, landed, dp_send.at[k], dp_recv.at[k], partner))
    for copy in dp_copies:
        copy.wait_recv()
    for copy in row_copies + dp_copies:
        copy.wait_send()


def gather_inputs(own):
    size = lax.axis_size("row")
    dma = pltpu.SemaphoreType.DMA
    return comm_call(
        gather_kernel,
        "gather_inputs",
        0,
        jax.ShapeDtypeStruct((2 * size,) + own.shape, own.dtype),
        [dma((size,)), dma((size,)), dma((size,)), dma((size,))],
        (own,),
    )


def hidden_kernel(
    pieces,
    part_ref,
    h_ref,
    from_dp,
    mine,
    from_col,
    dp_send,
    dp_recv,
    col_send,
    col_recv,
    last_send,
    last_recv,
):
    share = lax.axis_index("dp")
    peers, partner = others("col"), others("dp")[0]
    depth = part_ref.shape[2] // pieces
    meet(peers + [partner])
    cuts = [pl.ds(c * depth, depth) for c in range(pieces)]
    dp_copies = [
        send(
            part_ref.at[1 - share, :, cut],
            from_dp.at[:, cut],
            dp_send.at[c],
            dp_recv.at[c],
            partner,
        )
        for c, cut in enumerate(cuts)
    ]
    col_copies = []
    for c, cut in enumerate(cuts):
        dp_copies[c].wait_recv()
        total = part_ref[share, :, cut].astype(jnp.float32) + from_dp[:, cut].astype(jnp.float32)
        mine[:, cut] = total.astype(jnp.bfloat16)
        col_copies.append(
            [
                send(
                    mine.at[:, cut],
                    from_col.at[k, :, cut],
                    col_send.at[c, k],
                    col_recv.at[c, k],
                    peer,
                )
                for k, peer in enumerate(peers)
            ]
        )
    last_copies = []
    for c, cut in enumerate(cuts):
        total = mine[:, cut].astype(jnp.float32)
        for k, copy in enumerate(col_copies[c]):
            copy.wait_recv()
            total = total + from_col[k, :, cut].astype(jnp.float32)
        activation, slope = silu_pair(total[0])
        h_ref[share, 0, cut] = activation.astype(jnp.bfloat16)
        h_ref[share, 1, cut] = (total[1] * slope).astype(jnp.bfloat16)
        done = h_ref.at[share, :, cut]
        last_copies.append(send(done, done, last_send.at[c], last_recv.at[c], partner))
    for copy in last_copies:
        copy.wait_recv()
    for copy in dp_copies + sum(col_copies, []) + last_copies:
        copy.wait_send()


def hidden_exchange(partial):
    pieces = largest_divisor(partial.shape[2], 6)
    peers = lax.axis_size("col") - 1
    dma = pltpu.SemaphoreType.DMA
    piece = partial.shape[1:]
    return comm_call(
        functools.partial(hidden_kernel, pieces),
        "hidden_exchange",
        1,
        jax.ShapeDtypeStruct(partial.shape, jnp.bfloat16),
        [
            pltpu.VMEM(piece, jnp.bfloat16),
            pltpu.VMEM(piece, jnp.bfloat16),
            pltpu.VMEM((peers,) + piece, jnp.bfloat16),
            dma((pieces,)),
            dma((pieces,)),
            dma((pieces, peers)),
            dma((pieces, peers)),
            dma((pieces,)),
            dma((pieces,)),
        ],
        (partial,),
    )


def final_kernel(
    sums_ref,
    up_rows,
    up_cols,
    down_rows,
    down_cols,
    mixed_ref,
    grad_ref,
    up_rows_out,
    up_cols_out,
    down_rows_out,
    down_cols_out,
    from_dp,
    to_row,
    from_row,
    f_dp,
    u_dp,
    f_own,
    u_own,
    f_row,
    u_col,
    dp_send,
    dp_recv,
    row_send,
    row_recv,
    max_send,
    max_recv,
    f_send,
    f_recv,
    u_send,
    u_recv,
):
    size, me, share = lax.axis_size("row"), lax.axis_index("row"), lax.axis_index("dp")
    peers, columns, partner = others("row"), others("col"), others("dp")[0]
    meet(peers + columns + [partner])
    targets = [lax.rem(me + k, size) for k in range(1, size)] + [me]
    dp_copies = [
        send(
            sums_ref.at[(1 - share) * size + target],
            from_dp.at[k],
            dp_send.at[k],
            dp_recv.at[k],
            partner,
        )
        for k, target in enumerate(targets)
    ]
    f_own[0] = up_rows[...]
    f_own[1] = down_cols[...]
    u_own[0] = up_cols[...]
    u_own[1] = down_rows[...]
    max_copies = [
        send(f_own, f_dp, max_send.at[0], max_recv.at[0], partner),
        send(u_own, u_dp, max_send.at[1], max_recv.at[1], partner),
    ]
    row_copies = []
    for k, target in enumerate(targets):
        dp_copies[k].wait_recv()
        total = sums_ref[share * size + target].astype(jnp.float32)
        total = total + from_dp[k].astype(jnp.float32)
        if k < size - 1:
            to_row[k] = total.astype(jnp.bfloat16)
            row_copies.append(
                send(to_row.at[k], from_row.at[k], row_send.at[k], row_recv.at[k], peers[k])
            )
    max_copies[0].wait_recv()
    max_copies[0].wait_send()
    f_own[...] = jnp.maximum(f_own[...], f_dp[...])
    max_copies[1].wait_recv()
    max_copies[1].wait_send()
    u_own[...] = jnp.maximum(u_own[...], u_dp[...])
    f_copies = [
        send(f_own, f_row.at[k], f_send.at[k], f_recv.at[k], peer) for k, peer in enumerate(peers)
    ]
    u_copies = [
        send(u_own, u_col.at[k], u_send.at[k], u_recv.at[k], peer) for k, peer in enumerate(columns)
    ]
    best = u_own[...]
    for k, copy in enumerate(u_copies):
        copy.wait_recv()
        best = jnp.maximum(best, u_col[k])
    up_cols_out[...] = best[0]
    down_rows_out[...] = best[1]
    for k, copy in enumerate(row_copies):
        copy.wait_recv()
        total = total + from_row[k].astype(jnp.float32)
    half = mixed_ref.shape[0]
    mixed_ref[...] = total[:half].astype(jnp.bfloat16)
    grad_ref[...] = total[half:].astype(jnp.bfloat16)
    best = f_own[...]
    for k, copy in enumerate(f_copies):
        copy.wait_recv()
        best = jnp.maximum(best, f_row[k])
    up_rows_out[...] = best[0]
    down_cols_out[...] = best[1]
    for copy in dp_copies + row_copies + f_copies + u_copies:
        copy.wait_send()


def final_exchange(sums, *largest):
    size, columns = lax.axis_size("row"), lax.axis_size("col")
    dma = pltpu.SemaphoreType.DMA
    f32, bf16 = jnp.float32, jnp.bfloat16
    piece = sums.shape[1:]
    f_shape = (2,) + largest[0].shape
    u_shape = (2,) + largest[1].shape
    half = jax.ShapeDtypeStruct((piece[0] // 2, piece[1]), bf16)
    return comm_call(
        final_kernel,
        "final_exchange",
        2,
        (
            half,
            half,
            *[jax.ShapeDtypeStruct(value.shape, f32) for value in largest],
        ),
        [
            pltpu.VMEM((size,) + piece, bf16),
            pltpu.VMEM((size - 1,) + piece, bf16),
            pltpu.VMEM((size - 1,) + piece, bf16),
            pltpu.VMEM(f_shape, f32),
            pltpu.VMEM(u_shape, f32),
            pltpu.VMEM(f_shape, f32),
            pltpu.VMEM(u_shape, f32),
            pltpu.VMEM((size - 1,) + f_shape, f32),
            pltpu.VMEM((columns - 1,) + u_shape, f32),
            dma((size,)),
            dma((size,)),
            dma((size - 1,)),
            dma((size - 1,)),
            dma((2,)),
            dma((2,)),
            dma((size - 1,)),
            dma((size - 1,)),
            dma((columns - 1,)),
            dma((columns - 1,)),
        ],
        (sums, *largest),
    )


def on_device(
    tokens,
    cotangent,
    up_blocks,
    down_blocks,
    up_index,
    down_index,
    tile_counts,
    up_cover_rows,
    up_cover_cols,
    down_cover_rows,
    down_cover_cols,
):
    width = up_blocks.shape[-1]
    own_tokens = tokens.shape[0]
    features = tokens.shape[1] // width
    units = up_cover_cols.shape[0] // width
    shares = lax.axis_size("dp")
    rows = lax.axis_size("row")
    all_tokens = own_tokens * rows * shares

    up_at = up_index.reshape(-1)
    down_at = down_index.reshape(-1)
    counts = tile_counts.reshape(-1)
    place = lax.axis_index("dp").astype(jnp.int32).reshape(1)
    up_weight = up_blocks.reshape(up_blocks.shape[2:])
    down_weight = down_blocks.reshape(down_blocks.shape[2:])

    own = jnp.stack([tokens, cotangent]).reshape(2 * own_tokens * features, width)
    gathered = gather_inputs(own).reshape(shares * rows, 2, own_tokens, features, width)
    x = gathered.transpose(1, 3, 0, 2, 4).reshape(2, features, all_tokens, width)

    partial = first_products(
        up_at, down_at, counts, place, x, up_weight, down_weight, units, shares
    )
    h = hidden_exchange(partial)

    covers = [
        up_cover_rows.reshape(features, width),
        up_cover_cols.reshape(units, width),
        down_cover_rows.reshape(units, width),
        down_cover_cols.reshape(features, width),
    ]
    up_step, down_step, sums, *largest = second_products(
        up_at, down_at, counts, place, x, h, up_weight, down_weight, covers, shares
    )
    sums = sums.reshape(2, features, shares * rows, own_tokens, width).transpose(2, 0, 3, 1, 4)
    sums = sums.reshape(shares * rows, 2 * own_tokens * features, width)
    mixed, token_grad, *largest = final_exchange(sums, *largest)
    mixed = mixed.reshape(own_tokens, features * width)
    token_grad = token_grad.reshape(own_tokens, features * width)
    return (mixed, token_grad, up_step, down_step, *[value.reshape(-1) for value in largest])


def solution(mesh):
    in_specs = (
        P(("groups", "dp", "row"), "col"),
        P(("groups", "dp", "row"), "col"),
        P("row", "col", None, None, None),
        P("row", "col", None, None, None),
        P("row", "col", None, None),
        P("row", "col", None, None),
        P("row", "col", None),
        P("col"),
        P("row"),
        P("row"),
        P("col"),
    )
    out_specs = (
        P(("groups", "dp", "row"), "col"),
        P(("groups", "dp", "row"), "col"),
        P(("groups", "row"), "col", "dp", None, None),
        P(("groups", "row"), "col", "dp", None, None),
        P(("groups", "col")),
        P(("groups", "row")),
        P(("groups", "row")),
        P(("groups", "col")),
    )
    return jax.shard_map(
        on_device, mesh=mesh, in_specs=in_specs, out_specs=out_specs, check_vma=False
    )
```

```python
import functools

import jax
import jax.numpy as jnp
from jax import lax
from jax.experimental import pallas as pl
from jax.experimental.pallas import tpu as pltpu
from jax.sharding import PartitionSpec as P

MESH = pl.DeviceIdType.MESH
VMEM_LIMIT = 56 * 1024 * 1024
NN = (((1,), (0,)), ((), ()))
NT = (((1,), (1,)), ((), ()))


def largest_divisor(total, most):
    return max(d for d in range(1, most + 1) if total % d == 0)


def dot(left, right, dims):
    return lax.dot_general(left, right, dims, preferred_element_type=jnp.float32)


def slot_places(index_ref, slot, live, features, units):
    alive = slot < live
    read = index_ref[slot]
    feature = jnp.where(alive, read, features)
    unit = jnp.where(alive, index_ref[index_ref.shape[0] // 2 + slot], units)
    return read, feature, unit


def first_kernel(
    chunk, batch, up_at, down_at, counts, place, x_ref, up_ref, down_ref, out_ref, hid, dac
):
    step = pl.program_id(0)
    features = x_ref.shape[1]
    units = hid.shape[0] - 1
    shares, _, _, share_rows, _ = out_ref.shape

    @pl.when(step == 0)
    def _():
        hid[...] = jnp.zeros_like(hid)
        dac[...] = jnp.zeros_like(dac)

    first = place[0] * (chunk * pl.num_programs(0)) + step * chunk

    @pl.loop(0, chunk // batch)
    def _(part):
        work = []
        for j in range(batch):
            at = part * batch + j
            slot = first + at
            ux, uf, uu = slot_places(up_at, slot, counts[0], features, units)
            dx, df, du = slot_places(down_at, slot, counts[1], features, units)
            work.append((uu, dot(x_ref[0, ux], up_ref[at], NN), hid))
            work.append((du, dot(x_ref[1, dx], down_ref[at], NT), dac))
        for unit, product, total in work:
            total[unit] += product

    @pl.when(step == pl.num_programs(0) - 1)
    def _():
        for share in range(shares):
            rows = pl.ds(share * share_rows, share_rows)
            out_ref[share, 0] = hid[:units, rows, :].astype(jnp.bfloat16)
            out_ref[share, 1] = dac[:units, rows, :].astype(jnp.bfloat16)


def first_products(up_at, down_at, counts, place, x, up_weight, down_weight, units, shares):
    slots = up_weight.shape[0] // shares
    _, _, tokens, width = x.shape
    chunk = largest_divisor(slots, 48)
    batch = chunk
    steps = slots // chunk
    weight = pl.BlockSpec(
        (chunk, width, width), lambda i, a, b, c, p: (p[0] * steps + i, 0, 0)
    )
    return pl.pallas_call(
        functools.partial(first_kernel, chunk, batch),
        grid_spec=pltpu.PrefetchScalarGridSpec(
            num_scalar_prefetch=4,
            grid=(steps,),
            in_specs=[
                pl.BlockSpec(x.shape, lambda i, a, b, c, p: (0, 0, 0, 0)),
                weight,
                weight,
            ],
            out_specs=pl.BlockSpec(
                (shares, 2, units, tokens // shares, width), lambda i, a, b, c, p: (0, 0, 0, 0, 0)
            ),
            scratch_shapes=[
                pltpu.VMEM((units + 1, tokens, width), jnp.float32),
                pltpu.VMEM((units + 1, tokens, width), jnp.float32),
            ],
        ),
        out_shape=jax.ShapeDtypeStruct(
            (shares, 2, units, tokens // shares, width), jnp.bfloat16
        ),
        compiler_params=pltpu.CompilerParams(vmem_limit_bytes=VMEM_LIMIT),
        cost_estimate=pl.CostEstimate(
            flops=4 * slots * tokens * width * width,
            bytes_accessed=4 * slots * width * width,
            transcendentals=0,
        ),
    )(up_at, down_at, counts, place, x, up_weight, down_weight)


def second_kernel(
    chunk,
    batch,
    up_at,
    down_at,
    counts,
    place,
    x_ref,
    h_ref,
    up_ref,
    down_ref,
    up_rows,
    up_cols,
    down_rows,
    down_cols,
    up_step,
    down_step,
    sums_ref,
    up_rows_new,
    up_cols_new,
    down_rows_new,
    down_cols_new,
    x_turned,
    act_turned,
    dh,
    act,
    f_rows,
    u_rows,
    f_rows_max,
    u_rows_max,
    f_cols,
    u_cols,
    f_cols_max,
    u_cols_max,
    mix,
    tok,
):
    step = pl.program_id(0)
    features = x_ref.shape[1]
    shares, _, units, share_rows, _ = h_ref.shape
    width = x_ref.shape[-1]
    groups = width // 8

    @pl.when(step == 0)
    def _():
        mix[...] = jnp.zeros_like(mix)
        tok[...] = jnp.zeros_like(tok)
        dh[units] = jnp.zeros_like(dh[units])
        act[units] = jnp.zeros_like(act[units])
        act_turned[units] = jnp.zeros_like(act_turned[units])
        x_turned[features] = jnp.zeros_like(x_turned[features])
        f_rows[features] = jnp.ones_like(f_rows[features])
        u_rows[units] = jnp.ones_like(u_rows[units])
        f_cols[features] = jnp.ones_like(f_cols[features])
        u_cols[units] = jnp.ones_like(u_cols[units])
        f_cols_max[...] = jnp.zeros_like(f_cols_max)
        u_cols_max[...] = jnp.zeros_like(u_cols_max)

        @pl.loop(0, features, unroll=largest_divisor(features, 8))
        def _(f):
            x_turned[f] = x_ref[0, f].astype(jnp.float32).T.astype(jnp.bfloat16)
            wide = jnp.broadcast_to(up_rows[pl.ds(f, 1)], (width, width)).T
            f_rows[f] = wide
            f_rows_max[f] = wide
            f_cols[f] = down_cols[pl.ds(f, 1)]

        @pl.loop(0, units, unroll=largest_divisor(units, 8))
        def _(u):
            for share in range(shares):
                at = pl.ds(share * share_rows, share_rows)
                act[u, at] = h_ref[share, 0, u]
                dh[u, at] = h_ref[share, 1, u]
            act_turned[u] = act[u].astype(jnp.float32).T.astype(jnp.bfloat16)
            wide = jnp.broadcast_to(down_rows[pl.ds(u, 1)], (width, width)).T
            u_rows[u] = wide
            u_rows_max[u] = wide
            u_cols[u] = up_cols[pl.ds(u, 1)]

    first = place[0] * (chunk * pl.num_programs(0)) + step * chunk

    def one_step(grad, rows, cols, rows_max, cols_max, row, col, step_ref, at):
        second = jnp.minimum(rows[row], cols[col]) + grad * grad
        step_ref[0, 0, at] = (grad * lax.rsqrt(second)).astype(jnp.bfloat16)
        rows_max[row] = jnp.maximum(rows_max[row], second)
        best = jnp.max(second.reshape(groups, 8, width), axis=0)
        cols_max[col] = jnp.maximum(cols_max[col], best)

    @pl.loop(0, chunk // batch)
    def _(part):
        work = []
        for j in range(batch):
            at = part * batch + j
            slot = first + at
            ux, uf, uu = slot_places(up_at, slot, counts[0], features, units)
            dx, df, du = slot_places(down_at, slot, counts[1], features, units)
            work.append((uf, dot(dh[uu], up_ref[at], NT), tok))
            work.append((df, dot(act[du], down_ref[at], NN), mix))
        for feature, product, total in work:
            total[feature] += product
        for j in range(batch):
            at = part * batch + j
            slot = first + at
            ux, uf, uu = slot_places(up_at, slot, counts[0], features, units)
            dx, df, du = slot_places(down_at, slot, counts[1], features, units)
            up_grad = dot(x_turned[uf], dh[uu], NN)
            down_grad = dot(act_turned[du], x_ref[1, dx], NN)
            one_step(up_grad, f_rows, u_cols, f_rows_max, u_cols_max, uf, uu, up_step, at)
            one_step(down_grad, u_rows, f_cols, u_rows_max, f_cols_max, du, df, down_step, at)

    @pl.when(step == pl.num_programs(0) - 1)
    def _():
        sums_ref[0] = mix[:features].astype(jnp.bfloat16)
        sums_ref[1] = tok[:features].astype(jnp.bfloat16)

        @pl.loop(0, features, unroll=largest_divisor(features, 8))
        def _(f):
            up_rows_new[pl.ds(f, 1)] = jnp.max(f_rows_max[f].T, axis=0, keepdims=True)
            best = jnp.max(f_cols_max[f], axis=0, keepdims=True)
            down_cols_new[pl.ds(f, 1)] = jnp.maximum(best, f_cols[f])

        @pl.loop(0, units, unroll=largest_divisor(units, 8))
        def _(u):
            down_rows_new[pl.ds(u, 1)] = jnp.max(u_rows_max[u].T, axis=0, keepdims=True)
            best = jnp.max(u_cols_max[u], axis=0, keepdims=True)
            up_cols_new[pl.ds(u, 1)] = jnp.maximum(best, u_cols[u])


def second_products(
    up_at, down_at, counts, place, x, h, up_weight, down_weight, covers, shares
):
    slots = up_weight.shape[0] // shares
    _, features, tokens, width = x.shape
    units = h.shape[2]
    chunk = largest_divisor(slots, 48)
    batch = chunk
    steps = slots // chunk
    weight = pl.BlockSpec(
        (chunk, width, width), lambda i, a, b, c, p: (p[0] * steps + i, 0, 0)
    )
    stepped = pl.BlockSpec(
        (1, 1, chunk, width, width), lambda i, a, b, c, p: (0, 0, i, 0, 0)
    )

    def whole(shape):
        return pl.BlockSpec(shape, lambda i, a, b, c, p: (0,) * len(shape))

    f32, bf16 = jnp.float32, jnp.bfloat16
    sums = (2, features, tokens, width)
    return pl.pallas_call(
        functools.partial(second_kernel, chunk, batch),
        grid_spec=pltpu.PrefetchScalarGridSpec(
            num_scalar_prefetch=4,
            grid=(steps,),
            in_specs=[
                whole(x.shape),
                whole(h.shape),
                weight,
                weight,
                *[whole(cover.shape) for cover in covers],
            ],
            out_specs=[
                stepped,
                stepped,
                whole(sums),
                *[whole(cover.shape) for cover in covers],
            ],
            scratch_shapes=[
                pltpu.VMEM((features + 1, width, tokens), bf16),
                pltpu.VMEM((units + 1, width, tokens), bf16),
                pltpu.VMEM((units + 1, tokens, width), bf16),
                pltpu.VMEM((units + 1, tokens, width), bf16),
                pltpu.VMEM((features + 1, width, width), f32),
                pltpu.VMEM((units + 1, width, width), f32),
                pltpu.VMEM((features + 1, width, width), f32),
                pltpu.VMEM((units + 1, width, width), f32),
                pltpu.VMEM((features + 1, 1, width), f32),
                pltpu.VMEM((units + 1, 1, width), f32),
                pltpu.VMEM((features + 1, 8, width), f32),
                pltpu.VMEM((units + 1, 8, width), f32),
                pltpu.VMEM((features + 1, tokens, width), f32),
                pltpu.VMEM((features + 1, tokens, width), f32),
            ],
        ),
        out_shape=[
            jax.ShapeDtypeStruct((1, 1, slots, width, width), bf16),
            jax.ShapeDtypeStruct((1, 1, slots, width, width), bf16),
            jax.ShapeDtypeStruct(sums, bf16),
            *[jax.ShapeDtypeStruct(cover.shape, f32) for cover in covers],
        ],
        compiler_params=pltpu.CompilerParams(vmem_limit_bytes=VMEM_LIMIT),
        cost_estimate=pl.CostEstimate(
            flops=8 * slots * tokens * width * width,
            bytes_accessed=8 * slots * width * width,
            transcendentals=2 * slots * width * width,
        ),
    )(up_at, down_at, counts, place, x, h, up_weight, down_weight, *covers)


def silu_pair(hidden):
    sigma = 1.0 / (1.0 + jnp.exp(-hidden))
    return hidden * sigma, sigma * (1.0 + hidden * (1.0 - sigma))


def others(axis):
    size, me = lax.axis_size(axis), lax.axis_index(axis)
    return [{axis: lax.rem(me + k, size)} for k in range(1, size)]


def meet(devices):
    barrier = pltpu.get_barrier_semaphore()
    for device in devices:
        pl.semaphore_signal(barrier, inc=1, device_id=device, device_id_type=MESH)
    pl.semaphore_wait(barrier, len(devices))


def send(source, target, send_sem, recv_sem, device):
    copy = pltpu.make_async_remote_copy(
        src_ref=source,
        dst_ref=target,
        send_sem=send_sem,
        recv_sem=recv_sem,
        device_id=device,
        device_id_type=MESH,
    )
    copy.start()
    return copy


def comm_call(kernel, name, collective_id, out_shape, scratch_shapes, args):
    outs = jax.tree.map(lambda _: pl.BlockSpec(memory_space=pltpu.VMEM), out_shape)
    return pl.pallas_call(
        kernel,
        name=name,
        out_shape=out_shape,
        in_specs=[pl.BlockSpec(memory_space=pltpu.VMEM)] * len(args),
        out_specs=outs,
        scratch_shapes=scratch_shapes,
        compiler_params=pltpu.CompilerParams(
            collective_id=collective_id, has_side_effects=True, vmem_limit_bytes=VMEM_LIMIT
        ),
    )(*args)


def gather_kernel(own_ref, out_ref, row_send, row_recv, dp_send, dp_recv):
    size, me, share = lax.axis_size("row"), lax.axis_index("row"), lax.axis_index("dp")
    peers, partner = others("row"), others("dp")[0]
    meet(peers + [partner])
    mine = out_ref.at[share * size + me]
    row_copies = [
        send(own_ref, mine, row_send.at[k], row_recv.at[k], peer) for k, peer in enumerate(peers)
    ]
    dp_copies = [send(own_ref, mine, dp_send.at[size - 1], dp_recv.at[size - 1], partner)]
    out_ref[share * size + me] = own_ref[...]
    for k, copy in enumerate(row_copies):
        copy.wait_recv()
        landed = out_ref.at[share * size + lax.rem(me + size - k - 1, size)]
        dp_copies.append(send(landed, landed, dp_send.at[k], dp_recv.at[k], partner))
    for copy in dp_copies:
        copy.wait_recv()
    for copy in row_copies + dp_copies:
        copy.wait_send()


def gather_inputs(own):
    size = lax.axis_size("row")
    dma = pltpu.SemaphoreType.DMA
    return comm_call(
        gather_kernel,
        "gather_inputs",
        0,
        jax.ShapeDtypeStruct((2 * size,) + own.shape, own.dtype),
        [dma((size,)), dma((size,)), dma((size,)), dma((size,))],
        (own,),
    )


def hidden_kernel(
    pieces,
    part_ref,
    h_ref,
    from_dp,
    mine,
    from_col,
    dp_send,
    dp_recv,
    col_send,
    col_recv,
    last_send,
    last_recv,
):
    share = lax.axis_index("dp")
    peers, partner = others("col"), others("dp")[0]
    depth = part_ref.shape[2] // pieces
    meet(peers + [partner])
    cuts = [pl.ds(c * depth, depth) for c in range(pieces)]
    dp_copies = [
        send(
            part_ref.at[1 - share, :, cut],
            from_dp.at[:, cut],
            dp_send.at[c],
            dp_recv.at[c],
            partner,
        )
        for c, cut in enumerate(cuts)
    ]
    col_copies = []
    for c, cut in enumerate(cuts):
        dp_copies[c].wait_recv()
        total = part_ref[share, :, cut].astype(jnp.float32) + from_dp[:, cut].astype(jnp.float32)
        mine[:, cut] = total.astype(jnp.bfloat16)
        col_copies.append(
            [
                send(
                    mine.at[:, cut],
                    from_col.at[k, :, cut],
                    col_send.at[c, k],
                    col_recv.at[c, k],
                    peer,
                )
                for k, peer in enumerate(peers)
            ]
        )
    last_copies = []
    for c, cut in enumerate(cuts):
        total = mine[:, cut].astype(jnp.float32)
        for k, copy in enumerate(col_copies[c]):
            copy.wait_recv()
            total = total + from_col[k, :, cut].astype(jnp.float32)
        activation, slope = silu_pair(total[0])
        h_ref[share, 0, cut] = activation.astype(jnp.bfloat16)
        h_ref[share, 1, cut] = (total[1] * slope).astype(jnp.bfloat16)
        done = h_ref.at[share, :, cut]
        last_copies.append(send(done, done, last_send.at[c], last_recv.at[c], partner))
    for copy in last_copies:
        copy.wait_recv()
    for copy in dp_copies + sum(col_copies, []) + last_copies:
        copy.wait_send()


def hidden_exchange(partial):
    pieces = largest_divisor(partial.shape[2], 6)
    peers = lax.axis_size("col") - 1
    dma = pltpu.SemaphoreType.DMA
    piece = partial.shape[1:]
    return comm_call(
        functools.partial(hidden_kernel, pieces),
        "hidden_exchange",
        1,
        jax.ShapeDtypeStruct(partial.shape, jnp.bfloat16),
        [
            pltpu.VMEM(piece, jnp.bfloat16),
            pltpu.VMEM(piece, jnp.bfloat16),
            pltpu.VMEM((peers,) + piece, jnp.bfloat16),
            dma((pieces,)),
            dma((pieces,)),
            dma((pieces, peers)),
            dma((pieces, peers)),
            dma((pieces,)),
            dma((pieces,)),
        ],
        (partial,),
    )


def final_kernel(
    sums_ref,
    up_rows,
    up_cols,
    down_rows,
    down_cols,
    mixed_ref,
    grad_ref,
    up_rows_out,
    up_cols_out,
    down_rows_out,
    down_cols_out,
    from_dp,
    to_row,
    from_row,
    f_dp,
    u_dp,
    f_own,
    u_own,
    f_row,
    u_col,
    dp_send,
    dp_recv,
    row_send,
    row_recv,
    max_send,
    max_recv,
    f_send,
    f_recv,
    u_send,
    u_recv,
):
    size, me, share = lax.axis_size("row"), lax.axis_index("row"), lax.axis_index("dp")
    peers, columns, partner = others("row"), others("col"), others("dp")[0]
    meet(peers + columns + [partner])
    targets = [lax.rem(me + k, size) for k in range(1, size)] + [me]
    dp_copies = [
        send(
            sums_ref.at[(1 - share) * size + target],
            from_dp.at[k],
            dp_send.at[k],
            dp_recv.at[k],
            partner,
        )
        for k, target in enumerate(targets)
    ]
    f_own[0] = up_rows[...]
    f_own[1] = down_cols[...]
    u_own[0] = up_cols[...]
    u_own[1] = down_rows[...]
    max_copies = [
        send(f_own, f_dp, max_send.at[0], max_recv.at[0], partner),
        send(u_own, u_dp, max_send.at[1], max_recv.at[1], partner),
    ]
    row_copies = []
    for k, target in enumerate(targets):
        dp_copies[k].wait_recv()
        total = sums_ref[share * size + target].astype(jnp.float32)
        total = total + from_dp[k].astype(jnp.float32)
        if k < size - 1:
            to_row[k] = total.astype(jnp.bfloat16)
            row_copies.append(
                send(to_row.at[k], from_row.at[k], row_send.at[k], row_recv.at[k], peers[k])
            )
    max_copies[0].wait_recv()
    max_copies[0].wait_send()
    f_own[...] = jnp.maximum(f_own[...], f_dp[...])
    max_copies[1].wait_recv()
    max_copies[1].wait_send()
    u_own[...] = jnp.maximum(u_own[...], u_dp[...])
    f_copies = [
        send(f_own, f_row.at[k], f_send.at[k], f_recv.at[k], peer) for k, peer in enumerate(peers)
    ]
    u_copies = [
        send(u_own, u_col.at[k], u_send.at[k], u_recv.at[k], peer) for k, peer in enumerate(columns)
    ]
    best = u_own[...]
    for k, copy in enumerate(u_copies):
        copy.wait_recv()
        best = jnp.maximum(best, u_col[k])
    up_cols_out[...] = best[0]
    down_rows_out[...] = best[1]
    for k, copy in enumerate(row_copies):
        copy.wait_recv()
        total = total + from_row[k].astype(jnp.float32)
    half = mixed_ref.shape[0]
    mixed_ref[...] = total[:half]
    grad_ref[...] = total[half:]
    best = f_own[...]
    for k, copy in enumerate(f_copies):
        copy.wait_recv()
        best = jnp.maximum(best, f_row[k])
    up_rows_out[...] = best[0]
    down_cols_out[...] = best[1]
    for copy in dp_copies + row_copies + f_copies + u_copies:
        copy.wait_send()


def final_exchange(sums, *largest):
    size, columns = lax.axis_size("row"), lax.axis_size("col")
    dma = pltpu.SemaphoreType.DMA
    f32, bf16 = jnp.float32, jnp.bfloat16
    piece = sums.shape[1:]
    f_shape = (2,) + largest[0].shape
    u_shape = (2,) + largest[1].shape
    half = jax.ShapeDtypeStruct((piece[0] // 2, piece[1]), f32)
    return comm_call(
        final_kernel,
        "final_exchange",
        2,
        (
            half,
            half,
            *[jax.ShapeDtypeStruct(value.shape, f32) for value in largest],
        ),
        [
            pltpu.VMEM((size,) + piece, bf16),
            pltpu.VMEM((size - 1,) + piece, bf16),
            pltpu.VMEM((size - 1,) + piece, bf16),
            pltpu.VMEM(f_shape, f32),
            pltpu.VMEM(u_shape, f32),
            pltpu.VMEM(f_shape, f32),
            pltpu.VMEM(u_shape, f32),
            pltpu.VMEM((size - 1,) + f_shape, f32),
            pltpu.VMEM((columns - 1,) + u_shape, f32),
            dma((size,)),
            dma((size,)),
            dma((size - 1,)),
            dma((size - 1,)),
            dma((2,)),
            dma((2,)),
            dma((size - 1,)),
            dma((size - 1,)),
            dma((columns - 1,)),
            dma((columns - 1,)),
        ],
        (sums, *largest),
    )


def place_kernel(own_tokens, *refs):
    count = len(refs) // 2
    sources, targets = refs[:count], refs[count:]
    for source, target in zip(sources[:2], targets[:2]):
        features, width = source.shape[0] // own_tokens, source.shape[1]
        for f in range(features):
            rows = source[pl.ds(f, own_tokens, stride=features), :]
            target[:, pl.ds(f * width, width)] = rows.astype(target.dtype)
    for source, target in zip(sources[2:], targets[2:]):
        target[...] = source[...]


def place_outputs(own_tokens, mixed, token_grad, *largest):
    placed = jax.ShapeDtypeStruct((own_tokens, mixed.size // own_tokens), jnp.bfloat16)
    return pl.pallas_call(
        functools.partial(place_kernel, own_tokens),
        name="place_outputs",
        out_shape=[placed, placed, *[jax.ShapeDtypeStruct(v.shape, v.dtype) for v in largest]],
        in_specs=[pl.BlockSpec(memory_space=pltpu.VMEM)] * (2 + len(largest)),
        out_specs=[pl.BlockSpec(memory_space=pltpu.VMEM)] * (2 + len(largest)),
        compiler_params=pltpu.CompilerParams(vmem_limit_bytes=8 * 1024 * 1024),
    )(mixed, token_grad, *largest)


def on_device(
    tokens,
    cotangent,
    up_blocks,
    down_blocks,
    up_index,
    down_index,
    tile_counts,
    up_cover_rows,
    up_cover_cols,
    down_cover_rows,
    down_cover_cols,
):
    width = up_blocks.shape[-1]
    own_tokens = tokens.shape[0]
    features = tokens.shape[1] // width
    units = up_cover_cols.shape[0] // width
    shares = lax.axis_size("dp")
    rows = lax.axis_size("row")
    all_tokens = own_tokens * rows * shares

    up_at = up_index[0, 0].T.reshape(-1)
    down_at = down_index[0, 0].T.reshape(-1)
    counts = tile_counts.reshape(-1)
    place = lax.axis_index("dp").astype(jnp.int32).reshape(1)
    up_weight = up_blocks.reshape(up_blocks.shape[2:])
    down_weight = down_blocks.reshape(down_blocks.shape[2:])

    own = jnp.stack([tokens, cotangent]).reshape(2 * own_tokens * features, width)
    gathered = gather_inputs(own).reshape(shares * rows, 2, own_tokens, features, width)
    x = gathered.transpose(1, 3, 0, 2, 4).reshape(2, features, all_tokens, width)

    partial = first_products(
        up_at, down_at, counts, place, x, up_weight, down_weight, units, shares
    )
    h = hidden_exchange(partial)

    covers = [
        up_cover_rows.reshape(features, width),
        up_cover_cols.reshape(units, width),
        down_cover_rows.reshape(units, width),
        down_cover_cols.reshape(features, width),
    ]
    up_step, down_step, sums, *largest = second_products(
        up_at, down_at, counts, place, x, h, up_weight, down_weight, covers, shares
    )
    sums = sums.reshape(2, features, shares * rows, own_tokens, width).transpose(2, 0, 3, 1, 4)
    sums = sums.reshape(shares * rows, 2 * own_tokens * features, width)
    mixed, token_grad, *largest = final_exchange(sums, *largest)
    mixed, token_grad, *largest = place_outputs(own_tokens, mixed, token_grad, *largest)
    return (mixed, token_grad, up_step, down_step, *[value.reshape(-1) for value in largest])


def solution(mesh):
    in_specs = (
        P(("groups", "dp", "row"), "col"),
        P(("groups", "dp", "row"), "col"),
        P("row", "col", None, None, None),
        P("row", "col", None, None, None),
        P("row", "col", None, None),
        P("row", "col", None, None),
        P("row", "col", None),
        P("col"),
        P("row"),
        P("row"),
        P("col"),
    )
    out_specs = (
        P(("groups", "dp", "row"), "col"),
        P(("groups", "dp", "row"), "col"),
        P(("groups", "row"), "col", "dp", None, None),
        P(("groups", "row"), "col", "dp", None, None),
        P(("groups", "col")),
        P(("groups", "row")),
        P(("groups", "row")),
        P(("groups", "col")),
    )
    return jax.shard_map(
        on_device, mesh=mesh, in_specs=in_specs, out_specs=out_specs, check_vma=False
    )
```
